32 devices in a mesh: role: 4 (over x, core), fsdp: 8 (over z, y).
Axes of the slice: x: 2, y: 2, z: 4, core: 2. Of those that a mesh axis runs over, the one named last changes fastest.
Arguments:
- source_noise: bfloat16 [3072, 64], P('fsdp'), may hold values from -6 to 6
- score_noise: bfloat16 [3072, 64], P('fsdp'), may hold values from -6 to 6
- noise_level: float32 [3072], P('fsdp'), may hold values from 0.05 to 0.95
- embed_weight: bfloat16 [4, 64, 3072], P('role'), may hold values from -0.75 to 0.75
- time_vector: float32 [4, 3072], P('role'), may hold values from -6 to 6
- norm_gain: float32 [4, 3072], P('role'), may hold values from 0.5 to 1.5
- block_weight: bfloat16 [4, 3072, 1536], P('role', 'fsdp'), may hold values from -0.109375 to 0.109375
- readout_weight: bfloat16 [4, 1536, 64], P('role'), may hold values from -0.15625 to 0.15625
Outputs:
- grads: float32 [4, 3072, 1536], P('role', 'fsdp')
- generated: bfloat16 [3072, 64], P('fsdp')
The draws below stay inside these ranges and needn't reach their ends.
All inputs are finite; a program needn't handle non-finite values. Where the reference program divides by a largest or mean magnitude, that divisor is 1e-20 or more.
Results may differ from the reference program's by a relative error of at most 0.0065.
Values may be sent and summed in bfloat16 or wider, within the bound.
No kernel may reach another device: no remote copies, remote signals or barrier semaphores. Data moves between devices by JAX's collectives and lax.ppermute only.
A program may use at most 128 MiB of HBM per device.

```python
import math
import jax
import jax.numpy as jnp
from jax import lax

D = 3072
C = 64
F = 1536
TOKENS = 3072
GROUPS = 4


def block_levels(rng, shape, split, smallest, largest):
    factor_of, own = 1.0, jax.random.fold_in(rng, 6)
    for axis_at, parts in split:
        heights = jnp.exp(jax.random.uniform(jax.random.fold_in(own, axis_at), (parts,), jnp.float32, smallest / len(split), largest / len(split)))
        factor_of = factor_of * jnp.repeat(heights, shape[axis_at] // parts).reshape([-1 if axis == axis_at else 1 for axis in range(len(shape))])
    return factor_of


def normal_values(stream_key, extent, scale, bound, split=(), held_as=jnp.bfloat16):
    gain = block_levels(stream_key, extent, split, -0.22, 0.18) if split else 1.0
    array = jax.random.normal(stream_key, extent, jnp.float32) * scale * gain
    return jnp.minimum(jnp.maximum(array, -bound), bound).astype(held_as)


def setup_inputs(seed: int = 0) -> dict:
    arg_keys = jax.random.split(jax.random.key(seed), 9)
    return {
        "source_noise": normal_values(arg_keys[0], (TOKENS, C), 1.0, 6.0, ((0, 8),)),
        "score_noise": normal_values(arg_keys[1], (TOKENS, C), 1.0, 6.0, ((0, 8),)),
        "noise_level": jnp.clip(0.05 + 0.9 * jax.random.uniform(arg_keys[2], (TOKENS,), jnp.float32) ** block_levels(arg_keys[2], (TOKENS,), ((0, 8),), -0.2, 0.2), 0.05, 0.95),
        "embed_weight": normal_values(arg_keys[3], (GROUPS, C, D), C ** -0.5, 0.75, ((0, 4),)),
        "time_vector": normal_values(arg_keys[4], (GROUPS, D), 1.0, 6.0, ((0, 4),), jnp.float32),
        "norm_gain": jnp.clip(1.0 + 0.1 * jax.random.normal(arg_keys[5], (GROUPS, D), jnp.float32), 0.5, 1.5),
        "block_weight": normal_values(arg_keys[6], (GROUPS, D, F), D ** -0.5, 0.109375, ((0, 4), (1, 8))),
        "readout_weight": normal_values(arg_keys[7], (GROUPS, F, C), F ** -0.5, 0.15625, ((0, 4),)),
    }


adv_weight = 3.0

def norm_rows(preact, gain_row):
    return preact * lax.rsqrt(lax.optimization_barrier(jnp.mean(preact * preact, axis=-1, keepdims=True)) + 1e-06) * gain_row

def score_net(latent, level, embed_w, time_w, gain_row, block_w, readout_w):
    preact = jnp.dot(latent, embed_w, preferred_element_type=jnp.float32) + level[:, None] * time_w[None, :]
    normed = norm_rows(preact, gain_row).astype(jnp.bfloat16)
    hidden = jnp.dot(normed, block_w, preferred_element_type=jnp.float32)
    activated = jax.nn.gelu(hidden, approximate=True).astype(jnp.bfloat16)
    output = jnp.dot(activated, readout_w, preferred_element_type=jnp.float32).astype(jnp.bfloat16)
    return (preact, normed, hidden, output)

def hidden_grad(hidden, cotangent, readout_w):
    back = jnp.dot(cotangent, readout_w.astype(jnp.float32).T, precision=lax.Precision.HIGHEST)
    unused, gelu_back = jax.vjp(lambda value: jax.nn.gelu(value, approximate=True), hidden)
    return gelu_back(back)[0].astype(jnp.bfloat16)

def input_grad(hcot, preact, gain_row, block_w, embed_w):
    normed_back = jnp.dot(hcot, block_w.T, preferred_element_type=jnp.float32)
    unused, norm_back = jax.vjp(lambda value: norm_rows(value, gain_row), preact)
    pre_back = norm_back(normed_back)[0]
    return jnp.dot(pre_back, embed_w.astype(jnp.float32).T, precision=lax.Precision.HIGHEST)

def reference(source_noise, score_noise, noise_level, embed_weight, time_vector, norm_gain, block_weight, readout_weight):

    def params(index):
        return (embed_weight[index], time_vector[index], norm_gain[index], block_weight[index], readout_weight[index])
    ones = jnp.ones_like(noise_level)
    pre_gen, normed_gen, hidden_gen, generated = score_net(source_noise, ones, *params(0))
    level = noise_level[:, None]
    noised = ((1.0 - level) * generated.astype(jnp.float32) + level * score_noise.astype(jnp.float32)).astype(jnp.bfloat16)
    unused_a, unused_b, unused_c, real = score_net(noised, noise_level, *params(1))
    unused_d, normed_fake, hidden_fake, fake = score_net(noised, noise_level, *params(2))
    pre_critic, normed_critic, hidden_critic, critic = score_net(noised, noise_level, *params(3))
    gen32 = generated.astype(jnp.float32)
    real32 = real.astype(jnp.float32)
    fake32 = fake.astype(jnp.float32)
    spread = lax.optimization_barrier(jnp.mean(jnp.abs(gen32 - real32), axis=-1, keepdims=True)) + 1e-05
    dmd = ((fake32 - real32) / spread).astype(jnp.bfloat16)
    logit = lax.optimization_barrier(jnp.sum(critic.astype(jnp.float32), axis=-1, keepdims=True))
    adv_cot = jnp.broadcast_to(-jax.nn.sigmoid(-logit), critic.shape)
    adv_hcot = hidden_grad(hidden_critic, adv_cot, readout_weight[3])
    latent_back = input_grad(adv_hcot, pre_critic, norm_gain[3], block_weight[3], embed_weight[3])
    adversarial = (adv_weight * (1.0 - level) * latent_back).astype(jnp.bfloat16)
    push = dmd.astype(jnp.float32) + adversarial.astype(jnp.float32)
    factor = 1.0 / math.sqrt(TOKENS)

    def weight_grad(normed, hidden, cotangent, readout_w):
        hcot = hidden_grad(hidden, cotangent, readout_w)
        return jnp.dot(normed.T, hcot, preferred_element_type=jnp.float32) * factor
    grad_gen = weight_grad(normed_gen, hidden_gen, push, readout_weight[0])
    grad_fake = weight_grad(normed_fake, hidden_fake, fake32 - gen32, readout_weight[2])
    critic_cot = jnp.broadcast_to(jax.nn.sigmoid(logit), critic.shape)
    grad_critic = weight_grad(normed_critic, hidden_critic, critic_cot, readout_weight[3])
    grads = jnp.stack([grad_gen, jnp.zeros_like(grad_gen), grad_fake, grad_critic])
    return (grads, generated)
```

```python
import functools
import math

import jax
import jax.numpy as jnp
from jax import lax
from jax.experimental import pallas as pl
from jax.experimental.pallas import tpu as pltpu
from jax.sharding import PartitionSpec as P

adv_weight = 3.0
f32 = jnp.float32
bf16 = jnp.bfloat16
extra = 8
pieces = 2
part_limit = 54528
curve = math.sqrt(2.0 / math.pi)
bend = 0.044715


def halves(value):
    high = value.astype(bf16)
    return high, (value - high.astype(f32)).astype(bf16)


def mm(left, right, left_dim, right_dim):
    return lax.dot_general(
        left, right, (((left_dim,), (right_dim,)), ((), ())), preferred_element_type=f32
    )


def gelu_parts(hidden):
    square = hidden * hidden
    bent = jnp.tanh(curve * hidden * (1.0 + bend * square))
    return square, bent


def gelu_value(hidden, bent):
    return 0.5 * hidden * (1.0 + bent)


def gelu_slope(hidden, square, bent):
    return 0.5 * (1.0 + bent) + (0.5 * curve) * hidden * (1.0 - bent * bent) * (
        1.0 + (3.0 * bend) * square
    )


def level_rows(level):
    high = level.astype(bf16).astype(f32)
    mid = (level - high).astype(bf16).astype(f32)
    low = (level - high - mid).astype(bf16).astype(f32)
    row = lax.broadcasted_iota(jnp.int32, (extra, level.shape[1]), 0)
    return jnp.where(row == 0, high, jnp.where(row == 1, mid, jnp.where(row == 2, low, 0.0)))


def widen(latent, level):
    return jnp.concatenate([latent.astype(f32), level_rows(level)], axis=0)


def norm_scale(wide, gram, width):
    seen = lax.dot_general(
        gram,
        wide,
        (((1,), (0,)), ((), ())),
        precision=lax.Precision.HIGHEST,
        preferred_element_type=f32,
    )
    square = jnp.sum(seen * wide, axis=0, keepdims=True)
    return lax.rsqrt(square * (1.0 / width) + 1e-06), seen


def columns_of(at, half, upper):
    tile = half // pieces
    base = upper * half if at < pieces else (1 - upper) * half
    return pl.ds(pl.multiple_of(base + (at % pieces) * tile, tile), tile)


def part_kernel(embed_ref, vectors_ref, block_ref, *rest):
    *outs, embed, buffer, sems = rest
    place = lax.axis_index("fsdp")
    upper = place & 1
    depth, cols = buffer.shape
    half = cols // 2
    tile = half // pieces
    own = slice(None)
    if embed_ref.shape[1] != depth:
        own = pl.ds(pl.multiple_of(place * depth, depth), depth)
    small = pltpu.make_async_copy(embed_ref.at[:, own], embed, sems.at[2 * pieces])
    order = [*range(pieces, 2 * pieces), *range(pieces)]
    large = [
        pltpu.make_async_copy(
            block_ref.at[0, :, columns_of(at, half, upper)],
            buffer.at[:, at * tile : (at + 1) * tile],
            sems.at[at],
        )
        for at in order
    ]
    small.start()
    for copy in large:
        copy.start()
    stamp, gain = vectors_ref[0:1, own], vectors_ref[1:2, own]
    row = lax.broadcasted_iota(jnp.int32, (extra, depth), 0)
    stamped = jnp.where(row < 3, stamp * gain, 0.0)
    small.wait()
    gained = jnp.concatenate([embed[...].astype(f32) * gain, stamped], axis=0)
    rows = gained.shape[0]
    both = jnp.concatenate([gained, gained - gained.astype(bf16).astype(f32)], axis=0).astype(bf16)
    outs[2 * pieces][...] = both
    for at, copy in zip(order, large):
        copy.wait()
        part = mm(both, buffer[:, at * tile : (at + 1) * tile], 1, 0)
        outs[at][...] = (part[:rows] + part[rows:]).astype(outs[at].dtype)


def forward(wide, gram_ref, proj_refs, readout_ref, width, slope_ref=None):
    upper = lax.axis_index("fsdp") & 1
    half = proj_refs[0].shape[1] * pieces
    tile = half // pieces
    scale, seen = norm_scale(wide, gram_ref[...], width)
    wide16 = wide.astype(bf16)
    total = jnp.zeros((readout_ref.shape[0], wide.shape[1]), f32)
    for at, proj_ref in enumerate(proj_refs):
        hidden = scale * mm(proj_ref[...], wide16, 0, 0)
        square, bent = gelu_parts(hidden)
        activated = gelu_value(hidden, bent).astype(bf16)
        total = total + mm(readout_ref[:, columns_of(at, half, upper)], activated, 1, 0)
        if slope_ref is not None:
            slope_ref[at * tile : (at + 1) * tile, :] = gelu_slope(hidden, square, bent)
    return total.astype(bf16), scale, seen


def first_kernel(latent_ref, noise_ref, level_ref, gram_ref, *rest, width):
    *proj_refs, readout_ref, out_ref, mix_ref, gram_out_ref = rest
    channels, tokens = latent_ref.shape
    wide = widen(latent_ref[...], jnp.ones((1, tokens), f32))
    out_ref[...], unused, unused = forward(wide, gram_ref, proj_refs, readout_ref, width)
    level = level_ref[...]
    mix_ref[:channels, :] = level * noise_ref[...].astype(f32)
    mix_ref[channels:, :] = jnp.broadcast_to(level, (extra, tokens))
    gram_out_ref[...] = gram_ref[...]


def second_kernel(source_ref, own_ref, by1_ref, by2_ref, by3_ref, mix_ref, gram_ref, *rest, width):
    proj_refs = rest[: 2 * pieces]
    readout_ref, columns_ref, generated_ref, piece_ref, flat_ref, slope_ref, scaled_ref = rest[2 * pieces :]
    role, upper = lax.axis_index("role"), lax.axis_index("fsdp") & 1
    channels, tokens = source_ref.shape
    half = proj_refs[0].shape[1] * pieces
    tile = half // pieces
    level = mix_ref[channels : channels + 1, :]
    first = role == 0
    generated = jnp.where(
        first,
        own_ref[...].astype(f32),
        jnp.where(
            role == 3,
            by3_ref[...].astype(f32),
            jnp.where(role == 2, by2_ref[...].astype(f32), by1_ref[...].astype(f32)),
        ),
    )
    generated_ref[...] = generated.astype(bf16)
    noised = (1.0 - level) * generated + mix_ref[:channels, :]
    latent = jnp.where(first, source_ref[...].astype(f32), noised.astype(bf16).astype(f32))
    wide = widen(latent, jnp.where(first, 1.0, level))
    scores, scale, seen = forward(wide, gram_ref, proj_refs, readout_ref, width, slope_ref)
    piece_ref[...] = scores
    logit = jnp.sum(scores.astype(f32), axis=0, keepdims=True)
    flat_ref[...] = 1.0 / (1.0 + jnp.exp(-logit))

    @pl.when(role == 3)
    def _():
        high, low = halves(-1.0 / (1.0 + jnp.exp(logit)))
        cot = jnp.concatenate(
            [
                jnp.broadcast_to(high, (channels, tokens)),
                jnp.broadcast_to(low, (channels, tokens)),
            ],
            axis=0,
        )
        back_rows = jnp.zeros(wide.shape, f32)
        for at, proj_ref in enumerate(proj_refs):
            back = mm(columns_ref[columns_of(at, half, upper), :], cot, 1, 0)
            hcot = (back * slope_ref[at * tile : (at + 1) * tile, :]).astype(bf16)
            back_rows = back_rows + mm(proj_ref[...], hcot, 1, 0)
        inner = scale * jnp.sum(back_rows * wide, axis=0, keepdims=True)
        latent_back = scale * back_rows[:channels] - (scale * scale * inner * (1.0 / width)) * seen[:channels]
        piece_ref[...] = (adv_weight * (1.0 - level) * latent_back).astype(bf16)

    scaled = scale * wide
    scaled_ref[...] = jnp.concatenate([scaled, scaled - scaled.astype(bf16).astype(f32)], axis=0).astype(bf16)


def pull_back(cot, slope_ref, scaled_ref, columns_ref, out_refs, first_piece):
    upper = lax.axis_index("fsdp") & 1
    rows, tile = out_refs[0].shape
    half = tile * pieces
    scaled = scaled_ref[...]
    for at, out_ref in enumerate(out_refs, first_piece):
        back = mm(columns_ref[columns_of(at, half, upper), :], cot, 1, 0)
        hcot = (back * slope_ref[at * tile : (at + 1) * tile, :]).astype(bf16)
        part = mm(scaled, hcot, 1, 1)
        out_ref[...] = (part[:rows] + part[rows:]).astype(out_ref.dtype)


def send_kernel(
    adversarial_ref,
    real_ref,
    fake_ref,
    generated_ref,
    piece_ref,
    flat_ref,
    slope_ref,
    scaled_ref,
    columns_ref,
    cot_ref,
    *out_refs,
):
    role = lax.axis_index("role")
    first = role == 0
    generated = generated_ref[...].astype(f32)
    piece = piece_ref[...].astype(f32)
    fake = fake_ref[...].astype(f32)
    real = real_ref[...].astype(f32)
    adversarial = adversarial_ref[...].astype(f32)
    spread = jnp.mean(jnp.abs(generated - real), axis=0, keepdims=True) + 1e-05
    dmd = (fake - real) / spread
    flat = jnp.broadcast_to(flat_ref[...], generated.shape)
    flat_high = flat.astype(bf16).astype(f32)
    left = jnp.where(
        first, dmd, jnp.where(role == 2, piece, jnp.where(role == 3, flat_high, 0.0))
    ).astype(bf16)
    right = jnp.where(
        first,
        adversarial,
        jnp.where(role == 2, -generated, jnp.where(role == 3, flat - flat_high, 0.0)),
    ).astype(bf16)
    cot = jnp.concatenate([left, right], axis=0)
    cot_ref[...] = cot
    pull_back(cot, slope_ref, scaled_ref, columns_ref, out_refs, pieces)


def keep_kernel(cot_ref, slope_ref, scaled_ref, columns_ref, *out_refs):
    pull_back(cot_ref[...], slope_ref, scaled_ref, columns_ref, out_refs, 0)


def grad_kernel(own_ref, *rest, factor, keep):
    total_refs = rest[:pieces]
    *unused, out_ref, buffer, sems = rest[pieces:]
    upper = lax.axis_index("fsdp") & 1
    half = buffer.shape[1]
    tile = half // pieces
    own = own_ref[...]
    copies = []
    for at, total_ref in enumerate(total_refs):
        here = slice(at * tile, (at + 1) * tile)
        total = total_ref[...].astype(f32)
        part = mm(own, jnp.concatenate([total, total], axis=0).astype(bf16), 0, 0)
        buffer[:, here] = part * factor
        cols = columns_of(at if keep else at + pieces, half, upper)
        copy = pltpu.make_async_copy(buffer.at[:, here], out_ref.at[0, :, cols], sems.at[at])
        copy.start()
        copies.append(copy)
    for copy in copies:
        copy.wait()


def call(kernel, name, out_shape, inputs, scratch=(), cost=0):
    many = isinstance(out_shape, list)
    vmem = pl.BlockSpec(memory_space=pltpu.VMEM)
    return pl.pallas_call(
        kernel,
        out_shape=out_shape,
        in_specs=[vmem] * len(inputs),
        out_specs=[vmem] * len(out_shape) if many else vmem,
        scratch_shapes=list(scratch),
        compiler_params=pltpu.CompilerParams(vmem_limit_bytes=16 * 1024 * 1024),
        cost_estimate=pl.CostEstimate(flops=cost, bytes_accessed=cost // 1000, transcendentals=cost // 1000),
        name=name,
    )(*inputs)


def part_of(embed_w, vectors, block_weight):
    depth, cols = block_weight.shape[1:]
    channels = embed_w.shape[0]
    rows, half = channels + extra, cols // 2
    if depth % 128 != 0:
        embed_w, vectors = (
            lax.dynamic_slice_in_dim(value, lax.axis_index("fsdp") * depth, depth, 1)
            for value in (embed_w, vectors)
        )
    shapes = [jax.ShapeDtypeStruct((rows, half // pieces), dtype) for dtype in (f32, bf16) for at in range(pieces)]
    shapes.append(jax.ShapeDtypeStruct((2 * rows, depth), bf16))
    vmem = pl.BlockSpec(memory_space=pltpu.VMEM)
    hbm = pl.BlockSpec(memory_space=pltpu.HBM)
    return pl.pallas_call(
        part_kernel,
        out_shape=shapes,
        in_specs=[hbm, vmem, hbm],
        out_specs=[vmem] * len(shapes),
        scratch_shapes=[
            pltpu.VMEM((channels, depth), bf16),
            pltpu.VMEM((depth, cols), bf16),
            pltpu.SemaphoreType.DMA((2 * pieces + 1,)),
        ],
        compiler_params=pltpu.CompilerParams(vmem_limit_bytes=part_limit * 1024),
        cost_estimate=pl.CostEstimate(
            flops=8 * rows * depth * half, bytes_accessed=4 * depth * half, transcendentals=0
        ),
        name="part",
    )(embed_w, vectors, block_weight)


def gradient(own, totals, factor, cols, buffer=None):
    depth, half = own.shape[1], cols // 2
    keep = buffer is None
    vmem = pl.BlockSpec(memory_space=pltpu.VMEM)
    hbm = pl.BlockSpec(memory_space=pltpu.HBM)
    specs = [vmem] * (1 + pieces)
    inputs = [own, *totals]
    if not keep:
        specs.append(hbm)
        inputs.append(buffer)
    return pl.pallas_call(
        functools.partial(grad_kernel, factor=factor, keep=keep),
        out_shape=jax.ShapeDtypeStruct((1, depth, cols), f32),
        in_specs=specs,
        out_specs=hbm,
        input_output_aliases={} if keep else {len(inputs) - 1: 0},
        scratch_shapes=[pltpu.VMEM((depth, half), f32), pltpu.SemaphoreType.DMA((pieces,))],
        compiler_params=pltpu.CompilerParams(vmem_limit_bytes=16 * 1024 * 1024),
        cost_estimate=pl.CostEstimate(
            flops=4 * own.shape[0] * depth * half, bytes_accessed=4 * depth * half, transcendentals=0
        ),
        name="gradient_keep" if keep else "gradient_rest",
    )(*inputs)


def swap(values, axis, n, bit):
    pairs = [(i, i ^ bit) for i in range(n)]
    return [lax.ppermute(value, axis, pairs) for value in values]


def with_first(value, roles, other):
    pairs = [(0, other), (other, 0)] + [(i, i) for i in range(1, roles) if i != other]
    return lax.ppermute(value, "role", pairs)


def add_along(mine, received, n):
    mine = [value + part.astype(f32) for value, part in zip(mine, received)]
    bit = 2
    while bit < n:
        parts = swap([value.astype(bf16) for value in mine], "fsdp", n, bit)
        mine = [value + part.astype(f32) for value, part in zip(mine, parts)]
        bit *= 2
    return [value.astype(bf16) for value in mine]


def shards(
    source_noise,
    score_noise,
    noise_level,
    embed_weight,
    time_vector,
    norm_gain,
    block_weight,
    readout_weight,
):
    role = lax.axis_index("role")
    n = lax.axis_size("fsdp")
    embed_w = embed_weight[0]
    readout = readout_weight[0].T
    depth, cols = block_weight.shape[1:]
    channels, width = embed_w.shape
    tokens = source_noise.shape[0]
    rows = channels + extra
    half = cols // 2
    shape = jax.ShapeDtypeStruct
    roles = lax.axis_size("role")

    vectors = jnp.concatenate([time_vector, norm_gain], axis=0)
    *parts, own_rows = part_of(embed_w, vectors, block_weight)
    received = swap(parts[pieces:], "fsdp", n, 1)
    mine = add_along(parts[:pieces], received, n)
    proj = mine + swap(mine, "fsdp", n, 1)

    tall = jnp.concatenate(
        [embed_w.astype(f32), jnp.broadcast_to(time_vector, (3, width)), jnp.zeros((extra - 3, width), f32)]
    )
    gram = jnp.dot(tall, tall.T, precision=lax.Precision.HIGHEST)
    columns = jnp.concatenate([readout, readout], axis=0).T
    level = noise_level[None, :]
    source = source_noise.T
    latent_shape = shape((channels, tokens), bf16)

    own_first, mix, gram = call(
        functools.partial(first_kernel, width=width),
        "generator",
        [latent_shape, shape((rows, tokens), f32), shape((rows, rows), f32)],
        (source, score_noise.T, level, gram, *proj, readout),
    )
    by3, by2, by1 = (with_first(own_first, roles, other) for other in (3, 2, 1))
    drawn = jnp.where(role == 0, own_first, jnp.where(role == 1, by1, jnp.where(role == 2, by2, by3)))
    generated, piece, flat, slope, scaled = call(
        functools.partial(second_kernel, width=width),
        "score",
        [
            latent_shape,
            latent_shape,
            shape((1, tokens), f32),
            shape((cols, tokens), f32),
            shape((2 * rows, tokens), bf16),
        ],
        (source, own_first, by1, by2, by3, mix, gram, *proj, readout, columns),
    )
    real, fake, adversarial = (with_first(piece, roles, other) for other in (1, 2, 3))
    flat, drawn = lax.optimization_barrier((flat, drawn))

    cost = 4 * rows * tokens * half
    tail = (slope, scaled, columns)
    cot, *send = call(
        send_kernel,
        "cotangent_send",
        [shape((2 * channels, tokens), bf16)] + [shape((rows, half // pieces), bf16)] * pieces,
        (adversarial, real, fake, generated, piece, flat, *tail),
        cost=cost,
    )
    received = swap(send, "fsdp", n, 1)
    kept = call(
        keep_kernel, "cotangent_keep", [shape((rows, half // pieces), f32)] * pieces, (cot, *tail), cost=cost
    )
    totals = add_along(kept, received, n)
    others = swap(totals, "fsdp", n, 1)
    factor = 1.0 / math.sqrt(tokens * n)
    grads = gradient(own_rows, totals, factor, cols)
    grads = gradient(own_rows, others, factor, cols, grads)
    return (grads, drawn.T)


def solution(mesh):
    in_specs = (
        P("fsdp", None),
        P("fsdp", None),
        P("fsdp"),
        P("role", None, None),
        P("role", None),
        P("role", None),
        P("role", "fsdp", None),
        P("role", None, None),
    )
    out_specs = (P("role", "fsdp", None), P("fsdp", None))
    return jax.shard_map(shards, mesh=mesh, in_specs=in_specs, out_specs=out_specs, check_vma=False)
```

```python
import functools
import math

import jax
import jax.numpy as jnp
from jax import lax
from jax.experimental import pallas as pl
from jax.experimental.pallas import tpu as pltpu
from jax.sharding import PartitionSpec as P

adv_weight = 3.0
f32 = jnp.float32
bf16 = jnp.bfloat16
extra = 8
pieces = 2
part_limit = 54528
curve = math.sqrt(2.0 / math.pi)
bend = 0.044715


def halves(value):
    high = value.astype(bf16)
    return high, (value - high.astype(f32)).astype(bf16)


def mm(left, right, left_dim, right_dim):
    return lax.dot_general(
        left, right, (((left_dim,), (right_dim,)), ((), ())), preferred_element_type=f32
    )


def gelu_parts(hidden):
    square = hidden * hidden
    bent = jnp.tanh(curve * hidden * (1.0 + bend * square))
    return square, bent


def gelu_value(hidden, bent):
    return 0.5 * hidden * (1.0 + bent)


def gelu_slope(hidden, square, bent):
    return 0.5 * (1.0 + bent) + (0.5 * curve) * hidden * (1.0 - bent * bent) * (
        1.0 + (3.0 * bend) * square
    )


def level_rows(level):
    high = level.astype(bf16).astype(f32)
    mid = (level - high).astype(bf16).astype(f32)
    low = (level - high - mid).astype(bf16).astype(f32)
    row = lax.broadcasted_iota(jnp.int32, (extra, level.shape[1]), 0)
    return jnp.where(row == 0, high, jnp.where(row == 1, mid, jnp.where(row == 2, low, 0.0)))


def widen(latent, level):
    return jnp.concatenate([latent.astype(f32), level_rows(level)], axis=0)


def norm_scale(wide, gram, width):
    seen = lax.dot_general(
        gram,
        wide,
        (((1,), (0,)), ((), ())),
        precision=lax.Precision.HIGHEST,
        preferred_element_type=f32,
    )
    square = jnp.sum(seen * wide, axis=0, keepdims=True)
    return lax.rsqrt(square * (1.0 / width) + 1e-06), seen


def columns_of(at, half, upper):
    tile = half // pieces
    base = upper * half if at < pieces else (1 - upper) * half
    return pl.ds(pl.multiple_of(base + (at % pieces) * tile, tile), tile)


def part_kernel(embed_ref, vectors_ref, block_ref, *rest):
    *outs, embed, buffer, sems = rest
    place = lax.axis_index("fsdp")
    upper = place & 1
    depth, cols = buffer.shape
    half = cols // 2
    tile = half // pieces
    own = slice(None)
    if embed_ref.shape[1] != depth:
        own = pl.ds(pl.multiple_of(place * depth, depth), depth)
    small = pltpu.make_async_copy(embed_ref.at[:, own], embed, sems.at[2 * pieces])
    order = [*range(pieces, 2 * pieces), *range(pieces)]
    large = [
        pltpu.make_async_copy(
            block_ref.at[0, :, columns_of(at, half, upper)],
            buffer.at[:, at * tile : (at + 1) * tile],
            sems.at[at],
        )
        for at in order
    ]
    small.start()
    for copy in large:
        copy.start()
    stamp, gain = vectors_ref[0:1, own], vectors_ref[1:2, own]
    row = lax.broadcasted_iota(jnp.int32, (extra, depth), 0)
    stamped = jnp.where(row < 3, stamp * gain, 0.0)
    small.wait()
    gained = jnp.concatenate([embed[...].astype(f32) * gain, stamped], axis=0)
    rows = gained.shape[0]
    both = jnp.concatenate([gained, gained - gained.astype(bf16).astype(f32)], axis=0).astype(bf16)
    outs[2 * pieces][...] = both
    for at, copy in zip(order, large):
        copy.wait()
        part = mm(both, buffer[:, at * tile : (at + 1) * tile], 1, 0)
        outs[at][...] = (part[:rows] + part[rows:]).astype(outs[at].dtype)


def forward(wide, gram_ref, proj_refs, readout_ref, width, slope_ref=None):
    upper = lax.axis_index("fsdp") & 1
    half = proj_refs[0].shape[1] * pieces
    tile = half // pieces
    scale, seen = norm_scale(wide, gram_ref[...], width)
    wide16 = wide.astype(bf16)
    total = jnp.zeros((readout_ref.shape[0], wide.shape[1]), f32)
    for at, proj_ref in enumerate(proj_refs):
        hidden = scale * mm(proj_ref[...], wide16, 0, 0)
        square, bent = gelu_parts(hidden)
        activated = gelu_value(hidden, bent).astype(bf16)
        total = total + mm(readout_ref[:, columns_of(at, half, upper)], activated, 1, 0)
        if slope_ref is not None:
            slope_ref[at * tile : (at + 1) * tile, :] = gelu_slope(hidden, square, bent)
    return total.astype(bf16), scale, seen


def first_kernel(latent_ref, noise_ref, level_ref, gram_ref, *rest, width):
    *proj_refs, readout_ref, out_ref, mix_ref, gram_out_ref = rest
    channels, tokens = latent_ref.shape
    level = level_ref[...]
    mix_ref[:channels, :] = level * noise_ref[...].astype(f32)
    mix_ref[channels:, :] = jnp.broadcast_to(level, (extra, tokens))
    gram_out_ref[...] = gram_ref[...]

    @pl.when(lax.axis_index("role") == 0)
    def _():
        wide = widen(latent_ref[...], jnp.ones((1, tokens), f32))
        out_ref[...], unused, unused = forward(wide, gram_ref, proj_refs, readout_ref, width)


def in_parts(scale, wide):
    scaled = scale * wide
    return jnp.concatenate([scaled, scaled - scaled.astype(bf16).astype(f32)], axis=0).astype(bf16)


def slope_kernel(latent_ref, gram_ref, *rest, width):
    *proj_refs, slope_ref, scaled_ref = rest
    tile = proj_refs[0].shape[1]

    @pl.when(lax.axis_index("role") == 0)
    def _():
        wide = widen(latent_ref[...], jnp.ones((1, latent_ref.shape[1]), f32))
        scale, unused = norm_scale(wide, gram_ref[...], width)
        wide16 = wide.astype(bf16)
        for at, proj_ref in enumerate(proj_refs):
            hidden = scale * mm(proj_ref[...], wide16, 0, 0)
            square, bent = gelu_parts(hidden)
            slope_ref[at * tile : (at + 1) * tile, :] = gelu_slope(hidden, square, bent)
        scaled_ref[...] = in_parts(scale, wide)


def second_kernel(near_ref, far_ref, mix_ref, gram_ref, *rest, width):
    proj_refs = rest[: 2 * pieces]
    readout_ref, columns_ref, generated_ref, piece_ref, flat_ref, slope_ref, scaled_ref = rest[2 * pieces :]
    role, upper = lax.axis_index("role"), lax.axis_index("fsdp") & 1
    channels, tokens = near_ref.shape
    half = proj_refs[0].shape[1] * pieces
    tile = half // pieces
    generated = jnp.where(role < 2, near_ref[...].astype(f32), far_ref[...].astype(f32))
    generated_ref[...] = generated.astype(bf16)

    @pl.when(role > 0)
    def _():
        level = mix_ref[channels : channels + 1, :]
        noised = (1.0 - level) * generated + mix_ref[:channels, :]
        wide = widen(noised.astype(bf16), level)
        scores, scale, seen = forward(wide, gram_ref, proj_refs, readout_ref, width, slope_ref)
        piece_ref[...] = scores
        logit = jnp.sum(scores.astype(f32), axis=0, keepdims=True)
        flat_ref[...] = 1.0 / (1.0 + jnp.exp(-logit))
        scaled_ref[...] = in_parts(scale, wide)

        @pl.when(role == 3)
        def _():
            high, low = halves(-1.0 / (1.0 + jnp.exp(logit)))
            cot = jnp.concatenate(
                [
                    jnp.broadcast_to(high, (channels, tokens)),
                    jnp.broadcast_to(low, (channels, tokens)),
                ],
                axis=0,
            )
            back_rows = jnp.zeros(wide.shape, f32)
            for at, proj_ref in enumerate(proj_refs):
                back = mm(columns_ref[columns_of(at, half, upper), :], cot, 1, 0)
                hcot = (back * slope_ref[at * tile : (at + 1) * tile, :]).astype(bf16)
                back_rows = back_rows + mm(proj_ref[...], hcot, 1, 0)
            inner = scale * jnp.sum(back_rows * wide, axis=0, keepdims=True)
            latent_back = scale * back_rows[:channels] - (scale * scale * inner * (1.0 / width)) * seen[:channels]
            piece_ref[...] = (adv_weight * (1.0 - level) * latent_back).astype(bf16)


def pull_back(cot, tail, out_refs, first_piece):
    upper = lax.axis_index("fsdp") & 1
    first = lax.axis_index("role") == 0
    rows, tile = out_refs[0].shape
    half = tile * pieces
    columns_ref = tail[4]

    def with_slopes(slope_ref, scaled_ref):
        scaled = scaled_ref[...]
        for at, out_ref in enumerate(out_refs, first_piece):
            back = mm(columns_ref[columns_of(at, half, upper), :], cot, 1, 0)
            hcot = (back * slope_ref[at * tile : (at + 1) * tile, :]).astype(bf16)
            part = mm(scaled, hcot, 1, 1)
            out_ref[...] = (part[:rows] + part[rows:]).astype(out_ref.dtype)

    pl.when(first)(lambda: with_slopes(*tail[0:2]))
    pl.when(jnp.logical_not(first))(lambda: with_slopes(*tail[2:4]))


def send_kernel(
    real_ref,
    adversarial_ref,
    fake_ref,
    generated_ref,
    piece_ref,
    flat_ref,
    *rest,
):
    tail, cot_ref, out_refs = rest[:5], rest[5], rest[6:]
    role = lax.axis_index("role")
    first = role == 0
    generated = generated_ref[...].astype(f32)
    piece = piece_ref[...].astype(f32)
    fake = fake_ref[...].astype(f32)
    real = real_ref[...].astype(f32)
    adversarial = adversarial_ref[...].astype(f32)
    spread = jnp.mean(jnp.abs(generated - real), axis=0, keepdims=True) + 1e-05
    dmd = (fake - real) / spread
    flat = jnp.broadcast_to(flat_ref[...], generated.shape)
    flat_high = flat.astype(bf16).astype(f32)
    left = jnp.where(
        first, dmd, jnp.where(role == 2, piece, jnp.where(role == 3, flat_high, 0.0))
    ).astype(bf16)
    right = jnp.where(
        first,
        adversarial,
        jnp.where(role == 2, -generated, jnp.where(role == 3, flat - flat_high, 0.0)),
    ).astype(bf16)
    cot = jnp.concatenate([left, right], axis=0)
    cot_ref[...] = cot
    pull_back(cot, tail, out_refs, pieces)


def keep_kernel(cot_ref, *rest):
    pull_back(cot_ref[...], rest[:5], rest[5:], 0)


def grad_kernel(own_ref, *rest, factor, first_piece, count):
    total_refs = rest[:count]
    *unused, out_ref, buffer, sems = rest[count:]
    upper = lax.axis_index("fsdp") & 1
    tile = buffer.shape[1] // count
    own = own_ref[...]
    copies = []
    for at, total_ref in enumerate(total_refs):
        here = slice(at * tile, (at + 1) * tile)
        total = total_ref[...].astype(f32)
        part = mm(own, jnp.concatenate([total, total], axis=0).astype(bf16), 0, 0)
        buffer[:, here] = part * factor
        cols = columns_of(first_piece + at, tile * pieces, upper)
        copy = pltpu.make_async_copy(buffer.at[:, here], out_ref.at[0, :, cols], sems.at[at])
        copy.start()
        copies.append(copy)
    for copy in copies:
        copy.wait()


def call(kernel, name, out_shape, inputs, scratch=(), cost=0):
    many = isinstance(out_shape, list)
    vmem = pl.BlockSpec(memory_space=pltpu.VMEM)
    return pl.pallas_call(
        kernel,
        out_shape=out_shape,
        in_specs=[vmem] * len(inputs),
        out_specs=[vmem] * len(out_shape) if many else vmem,
        scratch_shapes=list(scratch),
        compiler_params=pltpu.CompilerParams(vmem_limit_bytes=16 * 1024 * 1024),
        cost_estimate=pl.CostEstimate(flops=cost, bytes_accessed=cost // 1000, transcendentals=cost // 1000),
        name=name,
    )(*inputs)


def part_of(embed_w, vectors, block_weight):
    depth, cols = block_weight.shape[1:]
    channels = embed_w.shape[0]
    rows, half = channels + extra, cols // 2
    if depth % 128 != 0:
        embed_w, vectors = (
            lax.dynamic_slice_in_dim(value, lax.axis_index("fsdp") * depth, depth, 1)
            for value in (embed_w, vectors)
        )
    shapes = [jax.ShapeDtypeStruct((rows, half // pieces), dtype) for dtype in (f32, bf16) for at in range(pieces)]
    shapes.append(jax.ShapeDtypeStruct((2 * rows, depth), bf16))
    vmem = pl.BlockSpec(memory_space=pltpu.VMEM)
    hbm = pl.BlockSpec(memory_space=pltpu.HBM)
    return pl.pallas_call(
        part_kernel,
        out_shape=shapes,
        in_specs=[hbm, vmem, hbm],
        out_specs=[vmem] * len(shapes),
        scratch_shapes=[
            pltpu.VMEM((channels, depth), bf16),
            pltpu.VMEM((depth, cols), bf16),
            pltpu.SemaphoreType.DMA((2 * pieces + 1,)),
        ],
        compiler_params=pltpu.CompilerParams(vmem_limit_bytes=part_limit * 1024),
        cost_estimate=pl.CostEstimate(
            flops=8 * rows * depth * half, bytes_accessed=4 * depth * half, transcendentals=0
        ),
        name="part",
    )(embed_w, vectors, block_weight)


def gradient(own, totals, first_piece, factor, cols, buffer=None):
    depth, tile, count = own.shape[1], cols // (2 * pieces), len(totals)
    vmem = pl.BlockSpec(memory_space=pltpu.VMEM)
    hbm = pl.BlockSpec(memory_space=pltpu.HBM)
    specs = [vmem] * (1 + count)
    inputs = [own, *totals]
    if buffer is not None:
        specs.append(hbm)
        inputs.append(buffer)
    return pl.pallas_call(
        functools.partial(grad_kernel, factor=factor, first_piece=first_piece, count=count),
        out_shape=jax.ShapeDtypeStruct((1, depth, cols), f32),
        in_specs=specs,
        out_specs=hbm,
        input_output_aliases={} if buffer is None else {len(inputs) - 1: 0},
        scratch_shapes=[pltpu.VMEM((depth, count * tile), f32), pltpu.SemaphoreType.DMA((count,))],
        compiler_params=pltpu.CompilerParams(vmem_limit_bytes=16 * 1024 * 1024),
        cost_estimate=pl.CostEstimate(
            flops=4 * own.shape[0] * depth * count * tile,
            bytes_accessed=4 * depth * count * tile,
            transcendentals=0,
        ),
        name="gradient",
    )(*inputs)


def swap(values, axis, n, bit):
    pairs = [(i, i ^ bit) for i in range(n)]
    return [lax.ppermute(value, axis, pairs) for value in values]


def add_along(mine, received, n):
    mine = [value + part.astype(f32) for value, part in zip(mine, received)]
    bit = 2
    while bit < n:
        parts = swap([value.astype(bf16) for value in mine], "fsdp", n, bit)
        mine = [value + part.astype(f32) for value, part in zip(mine, parts)]
        bit *= 2
    return [value.astype(bf16) for value in mine]


def shards(
    source_noise,
    score_noise,
    noise_level,
    embed_weight,
    time_vector,
    norm_gain,
    block_weight,
    readout_weight,
):
    role = lax.axis_index("role")
    n = lax.axis_size("fsdp")
    embed_w = embed_weight[0]
    readout = readout_weight[0].T
    depth, cols = block_weight.shape[1:]
    channels, width = embed_w.shape
    tokens = source_noise.shape[0]
    rows = channels + extra
    half = cols // 2
    shape = jax.ShapeDtypeStruct
    roles = lax.axis_size("role")

    vectors = jnp.concatenate([time_vector, norm_gain], axis=0)
    *parts, own_rows = part_of(embed_w, vectors, block_weight)
    received = swap(parts[pieces:], "fsdp", n, 1)
    mine = add_along(parts[:pieces], received, n)
    proj = mine + swap(mine, "fsdp", n, 1)

    tall = jnp.concatenate(
        [embed_w.astype(f32), jnp.broadcast_to(time_vector, (3, width)), jnp.zeros((extra - 3, width), f32)]
    )
    gram = jnp.dot(tall, tall.T, precision=lax.Precision.HIGHEST)
    columns = jnp.concatenate([readout, readout], axis=0).T
    level = noise_level[None, :]
    source = source_noise.T
    latent_shape = shape((channels, tokens), bf16)

    own_first, mix, gram = call(
        functools.partial(first_kernel, width=width),
        "generator",
        [latent_shape, shape((rows, tokens), f32), shape((rows, rows), f32)],
        (source, score_noise.T, level, gram, *proj, readout),
    )
    (by1,) = swap([own_first], "role", roles, 1)
    near = jnp.where(role == 1, by1, own_first)
    (by2,) = swap([near], "role", roles, 2)
    drawn = jnp.where(role < 2, near, by2)
    slope_shapes = [shape((cols, tokens), f32), shape((2 * rows, tokens), bf16)]
    first_slopes = call(
        functools.partial(slope_kernel, width=width),
        "slopes",
        slope_shapes,
        (source, gram, *proj),
        cost=2 * rows * tokens * cols,
    )
    generated, piece, flat, *slopes = call(
        functools.partial(second_kernel, width=width),
        "score",
        [
            latent_shape,
            latent_shape,
            shape((1, tokens), f32),
            *slope_shapes,
        ],
        (near, by2, mix, gram, *proj, readout, columns),
    )
    fake, adversarial, real = (swap([piece], "role", roles, bit)[0] for bit in (2, 3, 1))
    flat, drawn = lax.optimization_barrier((flat, drawn))

    cost = 4 * rows * tokens * half
    tail = (*first_slopes, *slopes, columns)
    cot, *send = call(
        send_kernel,
        "cotangent_send",
        [shape((2 * channels, tokens), bf16)] + [shape((rows, half // pieces), bf16)] * pieces,
        (real, adversarial, fake, generated, piece, flat, *tail),
        cost=cost,
    )
    received = swap(send, "fsdp", n, 1)
    kept = call(
        keep_kernel, "cotangent_keep", [shape((rows, half // pieces), f32)] * pieces, (cot, *tail), cost=cost
    )
    totals = add_along(kept, received, n)
    others = swap(totals, "fsdp", n, 1)
    factor = 1.0 / math.sqrt(tokens * n)
    grads = gradient(own_rows, totals, 0, factor, cols)
    for at, other in enumerate(others, pieces):
        grads = gradient(own_rows, [other], at, factor, cols, grads)
    return (grads, drawn.T)


def solution(mesh):
    in_specs = (
        P("fsdp", None),
        P("fsdp", None),
        P("fsdp"),
        P("role", None, None),
        P("role", None),
        P("role", None),
        P("role", "fsdp", None),
        P("role", None, None),
    )
    out_specs = (P("role", "fsdp", None), P("fsdp", None))
    return jax.shard_map(shards, mesh=mesh, in_specs=in_specs, out_specs=out_specs, check_vma=False)
```

```python
import functools
import math

import jax
import jax.numpy as jnp
from jax import lax
from jax.experimental import pallas as pl
from jax.experimental.pallas import tpu as pltpu
from jax.sharding import PartitionSpec as P

adv_weight = 3.0
f32 = jnp.float32
bf16 = jnp.bfloat16
extra = 8
chains = 2
part_limit = 54528
curve = math.sqrt(2.0 / math.pi)
bend = 0.044715


def halves(value):
    high = value.astype(bf16)
    return high, (value - high.astype(f32)).astype(bf16)


def mm(left, right, left_dim, right_dim):
    return lax.dot_general(
        left, right, (((left_dim,), (right_dim,)), ((), ())), preferred_element_type=f32
    )


def gelu_gate(hidden):
    square = hidden * hidden
    return 0.5 + 0.5 * jnp.tanh(hidden * (curve + (curve * bend) * square)), square


def gelu_slope(hidden, square, gate):
    return gate + (gate - gate * gate) * (hidden * (2.0 * curve + (6.0 * curve * bend) * square))


def level_rows(level):
    high = level.astype(bf16).astype(f32)
    mid = (level - high).astype(bf16).astype(f32)
    low = (level - high - mid).astype(bf16).astype(f32)
    row = lax.broadcasted_iota(jnp.int32, (extra, level.shape[1]), 0)
    return jnp.where(row == 0, high, jnp.where(row == 1, mid, jnp.where(row == 2, low, 0.0)))


def widen(latent, level):
    return jnp.concatenate([latent.astype(f32), level_rows(level)], axis=0)


def norm_scale(wide, gram, width):
    seen = lax.dot_general(
        gram,
        wide,
        (((1,), (0,)), ((), ())),
        precision=lax.Precision.HIGHEST,
        preferred_element_type=f32,
    )
    square = jnp.sum(seen * wide, axis=0, keepdims=True)
    return lax.rsqrt(square * (1.0 / width) + 1e-06), seen


def columns_of(at, tile):
    chain = at % chains
    kept = (lax.axis_index("fsdp") >> chain) & 1
    base = 2 * tile * chain + tile * (kept if at < chains else 1 - kept)
    return pl.ds(pl.multiple_of(base, tile), tile)


def part_kernel(embed_ref, vectors_ref, block_ref, *rest):
    *outs, embed, buffer, sems = rest
    place = lax.axis_index("fsdp")
    depth, cols = buffer.shape
    tile = cols // (2 * chains)
    own = slice(None)
    if embed_ref.shape[1] != depth:
        own = pl.ds(pl.multiple_of(place * depth, depth), depth)
    small = pltpu.make_async_copy(embed_ref.at[:, own], embed, sems.at[2 * chains])
    order = [*range(chains, 2 * chains), *range(chains)]
    large = [
        pltpu.make_async_copy(
            block_ref.at[0, :, columns_of(at, tile)],
            buffer.at[:, at * tile : (at + 1) * tile],
            sems.at[at],
        )
        for at in order
    ]
    small.start()
    for copy in large:
        copy.start()
    stamp, gain = vectors_ref[0:1, own], vectors_ref[1:2, own]
    row = lax.broadcasted_iota(jnp.int32, (extra, depth), 0)
    stamped = jnp.where(row < 3, stamp * gain, 0.0)
    small.wait()
    gained = jnp.concatenate([embed[...].astype(f32) * gain, stamped], axis=0)
    rows = gained.shape[0]
    both = jnp.concatenate([gained, gained - gained.astype(bf16).astype(f32)], axis=0).astype(bf16)
    outs[2 * chains][...] = both
    for at, copy in zip(order, large):
        copy.wait()
        part = mm(both, buffer[:, at * tile : (at + 1) * tile], 1, 0)
        outs[at][...] = (part[:rows] + part[rows:]).astype(outs[at].dtype)


def network(wide16, scale, proj_refs, first_piece, readout_ref, slope_ref=None):
    tile = proj_refs[0].shape[1]
    total = jnp.zeros((readout_ref.shape[0], wide16.shape[1]), f32)
    for at, proj_ref in enumerate(proj_refs, first_piece):
        hidden = scale * mm(proj_ref[...], wide16, 0, 0)
        gate, square = gelu_gate(hidden)
        activated = (hidden * gate).astype(bf16)
        total = total + mm(readout_ref[:, columns_of(at, tile)], activated, 1, 0)
        if slope_ref is not None:
            slope_ref[at * tile : (at + 1) * tile, :] = gelu_slope(hidden, square, gate)
    return total


def early_kernel(latent_ref, gram_ref, *rest, width):
    *proj_refs, readout_ref, total_ref = rest
    channels, tokens = latent_ref.shape

    @pl.when(lax.axis_index("role") == 0)
    def _():
        wide = widen(latent_ref[...], jnp.ones((1, tokens), f32))
        scale, unused = norm_scale(wide, gram_ref[...], width)
        total_ref[:channels, :] = network(wide.astype(bf16), scale, proj_refs, 0, readout_ref)
        total_ref[channels:, :] = jnp.broadcast_to(scale, (extra, tokens))


def late_kernel(latent_ref, noise_ref, level_ref, gram_ref, total_ref, *rest):
    *proj_refs, readout_ref, out_ref, mix_ref, gram_out_ref = rest
    channels, tokens = latent_ref.shape
    level = level_ref[...]
    mix_ref[:channels, :] = level * noise_ref[...].astype(f32)
    mix_ref[channels:, :] = jnp.broadcast_to(level, (extra, tokens))
    gram_out_ref[...] = gram_ref[...]

    @pl.when(lax.axis_index("role") == 0)
    def _():
        wide16 = widen(latent_ref[...], jnp.ones((1, tokens), f32)).astype(bf16)
        scale = total_ref[channels : channels + 1, :]
        total = network(wide16, scale, proj_refs, chains, readout_ref)
        out_ref[...] = (total_ref[:channels, :] + total).astype(bf16)


def in_parts(scale, wide):
    scaled = scale * wide
    return jnp.concatenate([scaled, scaled - scaled.astype(bf16).astype(f32)], axis=0).astype(bf16)


def slope_kernel(latent_ref, gram_ref, *rest, width):
    *proj_refs, slope_ref, scaled_ref = rest
    tile = proj_refs[0].shape[1]

    @pl.when(lax.axis_index("role") == 0)
    def _():
        wide = widen(latent_ref[...], jnp.ones((1, latent_ref.shape[1]), f32))
        scale, unused = norm_scale(wide, gram_ref[...], width)
        wide16 = wide.astype(bf16)
        for at, proj_ref in enumerate(proj_refs):
            hidden = scale * mm(proj_ref[...], wide16, 0, 0)
            gate, square = gelu_gate(hidden)
            slope_ref[at * tile : (at + 1) * tile, :] = gelu_slope(hidden, square, gate)
        scaled_ref[...] = in_parts(scale, wide)


def second_kernel(even_ref, odd_ref, mix_ref, gram_ref, *rest, width):
    proj_refs = rest[: 2 * chains]
    readout_ref, columns_ref, generated_ref, piece_ref, flat_ref, slope_ref, scaled_ref = rest[2 * chains :]
    role = lax.axis_index("role")
    channels, tokens = even_ref.shape
    tile = proj_refs[0].shape[1]
    generated = jnp.where((role & 1) == 0, even_ref[...].astype(f32), odd_ref[...].astype(f32))
    generated_ref[...] = generated.astype(bf16)

    @pl.when(role > 0)
    def _():
        level = mix_ref[channels : channels + 1, :]
        noised = (1.0 - level) * generated + mix_ref[:channels, :]
        wide = widen(noised.astype(bf16), level)
        scale, seen = norm_scale(wide, gram_ref[...], width)
        scores = network(wide.astype(bf16), scale, proj_refs, 0, readout_ref, slope_ref).astype(bf16)
        piece_ref[...] = scores
        logit = jnp.sum(scores.astype(f32), axis=0, keepdims=True)
        flat_ref[...] = 1.0 / (1.0 + jnp.exp(-logit))
        scaled_ref[...] = in_parts(scale, wide)

        @pl.when(role == 3)
        def _():
            high, low = halves(-1.0 / (1.0 + jnp.exp(logit)))
            cot = jnp.concatenate(
                [
                    jnp.broadcast_to(high, (channels, tokens)),
                    jnp.broadcast_to(low, (channels, tokens)),
                ],
                axis=0,
            )
            back_rows = jnp.zeros(wide.shape, f32)
            for at, proj_ref in enumerate(proj_refs):
                back = mm(columns_ref[columns_of(at, tile), :], cot, 1, 0)
                hcot = (back * slope_ref[at * tile : (at + 1) * tile, :]).astype(bf16)
                back_rows = back_rows + mm(proj_ref[...], hcot, 1, 0)
            inner = scale * jnp.sum(back_rows * wide, axis=0, keepdims=True)
            latent_back = scale * back_rows[:channels] - (scale * scale * inner * (1.0 / width)) * seen[:channels]
            piece_ref[...] = (adv_weight * (1.0 - level) * latent_back).astype(bf16)


def pull_back(cot, tail, out_refs, first_piece):
    first = lax.axis_index("role") == 0
    rows, tile = out_refs[0].shape
    columns_ref = tail[4]

    def with_slopes(slope_ref, scaled_ref):
        scaled = scaled_ref[...]
        for at, out_ref in enumerate(out_refs, first_piece):
            back = mm(columns_ref[columns_of(at, tile), :], cot, 1, 0)
            hcot = (back * slope_ref[at * tile : (at + 1) * tile, :]).astype(bf16)
            part = mm(scaled, hcot, 1, 1)
            out_ref[...] = (part[:rows] + part[rows:]).astype(out_ref.dtype)

    pl.when(first)(lambda: with_slopes(*tail[0:2]))
    pl.when(jnp.logical_not(first))(lambda: with_slopes(*tail[2:4]))


def send_kernel(
    real_ref,
    adversarial_ref,
    fake_ref,
    generated_ref,
    piece_ref,
    flat_ref,
    *rest,
):
    tail, cot_ref, out_refs = rest[:5], rest[5], rest[6:]
    role = lax.axis_index("role")
    first = role == 0
    generated = generated_ref[...].astype(f32)
    piece = piece_ref[...].astype(f32)
    fake = fake_ref[...].astype(f32)
    real = real_ref[...].astype(f32)
    adversarial = adversarial_ref[...].astype(f32)
    spread = jnp.mean(jnp.abs(generated - real), axis=0, keepdims=True) + 1e-05
    dmd = (fake - real) / spread
    flat = jnp.broadcast_to(flat_ref[...], generated.shape)
    flat_high = flat.astype(bf16).astype(f32)
    left = jnp.where(
        first, dmd, jnp.where(role == 2, piece, jnp.where(role == 3, flat_high, 0.0))
    ).astype(bf16)
    right = jnp.where(
        first,
        adversarial,
        jnp.where(role == 2, -generated, jnp.where(role == 3, flat - flat_high, 0.0)),
    ).astype(bf16)
    cot = jnp.concatenate([left, right], axis=0)
    cot_ref[...] = cot
    pull_back(cot, tail, out_refs, chains)


def keep_kernel(cot_ref, *rest):
    pull_back(cot_ref[...], rest[:5], rest[5:], 0)


def grad_kernel(own_ref, *rest, factor, first_piece, count):
    total_refs = rest[:count]
    *unused, out_ref, buffer, sems = rest[count:]
    tile = buffer.shape[1] // count
    own = own_ref[...]
    copies = []
    for at, total_ref in enumerate(total_refs):
        here = slice(at * tile, (at + 1) * tile)
        total = total_ref[...].astype(f32)
        part = mm(own, jnp.concatenate([total, total], axis=0).astype(bf16), 0, 0)
        buffer[:, here] = part * factor
        cols = columns_of(first_piece + at, tile)
        copy = pltpu.make_async_copy(buffer.at[:, here], out_ref.at[0, :, cols], sems.at[at])
        copy.start()
        copies.append(copy)
    for copy in copies:
        copy.wait()


def call(kernel, name, out_shape, inputs, scratch=(), cost=0):
    many = isinstance(out_shape, list)
    vmem = pl.BlockSpec(memory_space=pltpu.VMEM)
    return pl.pallas_call(
        kernel,
        out_shape=out_shape,
        in_specs=[vmem] * len(inputs),
        out_specs=[vmem] * len(out_shape) if many else vmem,
        scratch_shapes=list(scratch),
        compiler_params=pltpu.CompilerParams(vmem_limit_bytes=16 * 1024 * 1024),
        cost_estimate=pl.CostEstimate(flops=cost, bytes_accessed=cost // 1000, transcendentals=cost // 1000),
        name=name,
    )(*inputs)


def part_of(embed_w, vectors, block_weight):
    depth, cols = block_weight.shape[1:]
    channels = embed_w.shape[0]
    rows, tile = channels + extra, cols // (2 * chains)
    if depth % 128 != 0:
        embed_w, vectors = (
            lax.dynamic_slice_in_dim(value, lax.axis_index("fsdp") * depth, depth, 1)
            for value in (embed_w, vectors)
        )
    shapes = [jax.ShapeDtypeStruct((rows, tile), dtype) for dtype in (f32, bf16) for at in range(chains)]
    shapes.append(jax.ShapeDtypeStruct((2 * rows, depth), bf16))
    vmem = pl.BlockSpec(memory_space=pltpu.VMEM)
    hbm = pl.BlockSpec(memory_space=pltpu.HBM)
    return pl.pallas_call(
        part_kernel,
        out_shape=shapes,
        in_specs=[hbm, vmem, hbm],
        out_specs=[vmem] * len(shapes),
        scratch_shapes=[
            pltpu.VMEM((channels, depth), bf16),
            pltpu.VMEM((depth, cols), bf16),
            pltpu.SemaphoreType.DMA((2 * chains + 1,)),
        ],
        compiler_params=pltpu.CompilerParams(vmem_limit_bytes=part_limit * 1024),
        cost_estimate=pl.CostEstimate(
            flops=4 * rows * depth * cols, bytes_accessed=2 * depth * cols, transcendentals=0
        ),
        name="part",
    )(embed_w, vectors, block_weight)


def gradient(own, totals, first_piece, factor, cols, buffer=None):
    depth, tile, count = own.shape[1], cols // (2 * chains), len(totals)
    vmem = pl.BlockSpec(memory_space=pltpu.VMEM)
    hbm = pl.BlockSpec(memory_space=pltpu.HBM)
    specs = [vmem] * (1 + count)
    inputs = [own, *totals]
    if buffer is not None:
        specs.append(hbm)
        inputs.append(buffer)
    return pl.pallas_call(
        functools.partial(grad_kernel, factor=factor, first_piece=first_piece, count=count),
        out_shape=jax.ShapeDtypeStruct((1, depth, cols), f32),
        in_specs=specs,
        out_specs=hbm,
        input_output_aliases={} if buffer is None else {len(inputs) - 1: 0},
        scratch_shapes=[pltpu.VMEM((depth, count * tile), f32), pltpu.SemaphoreType.DMA((count,))],
        compiler_params=pltpu.CompilerParams(vmem_limit_bytes=16 * 1024 * 1024),
        cost_estimate=pl.CostEstimate(
            flops=4 * own.shape[0] * depth * count * tile,
            bytes_accessed=4 * depth * count * tile,
            transcendentals=0,
        ),
        name="gradient",
    )(*inputs)


def swap(value, axis, n, bit):
    return lax.ppermute(value, axis, [(i, i ^ bit) for i in range(n)])


def add_all(kept, sent, n):
    bits = [1 << at for at in range(n.bit_length() - 1)]
    orders = [[1, *reversed(bits[1:])], [2, 1, *bits[2:]]]
    mine = []
    for value, part, order in zip(kept, sent, orders):
        for step, bit in enumerate(order):
            outgoing = value.astype(bf16) if step else part
            value = value + swap(outgoing, "fsdp", n, bit).astype(f32)
        mine.append(value.astype(bf16))
    others = [swap(value, "fsdp", n, order[0]) for value, order in zip(mine, orders)]
    return mine, others


def shards(
    source_noise,
    score_noise,
    noise_level,
    embed_weight,
    time_vector,
    norm_gain,
    block_weight,
    readout_weight,
):
    role = lax.axis_index("role")
    n = lax.axis_size("fsdp")
    embed_w = embed_weight[0]
    readout = readout_weight[0].T
    depth, cols = block_weight.shape[1:]
    channels, width = embed_w.shape
    tokens = source_noise.shape[0]
    rows = channels + extra
    tile = cols // (2 * chains)
    shape = jax.ShapeDtypeStruct
    roles = lax.axis_size("role")

    vectors = jnp.concatenate([time_vector, norm_gain], axis=0)
    *parts, own_rows = part_of(embed_w, vectors, block_weight)
    mine, others = add_all(parts[:chains], parts[chains:], n)
    proj = mine + others

    tall = jnp.concatenate(
        [embed_w.astype(f32), jnp.broadcast_to(time_vector, (3, width)), jnp.zeros((extra - 3, width), f32)]
    )
    gram = jnp.dot(tall, tall.T, precision=lax.Precision.HIGHEST)
    columns = jnp.concatenate([readout, readout], axis=0).T
    level = noise_level[None, :]
    source = source_noise.T
    latent_shape = shape((channels, tokens), bf16)

    cost = 2 * rows * tokens * cols
    total = call(
        functools.partial(early_kernel, width=width),
        "generator_early",
        shape((rows, tokens), f32),
        (source, gram, *mine, readout),
        cost=cost,
    )
    own_first, mix, gram = call(
        late_kernel,
        "generator_late",
        [latent_shape, shape((rows, tokens), f32), shape((rows, rows), f32)],
        (source, score_noise.T, level, gram, total, *others, readout),
    )
    by2 = swap(own_first, "role", roles, 2)
    even = jnp.where(role == 2, by2, own_first)
    by1 = swap(even, "role", roles, 1)
    drawn = jnp.where(role % 2 == 0, even, by1)
    slope_shapes = [shape((cols, tokens), f32), shape((2 * rows, tokens), bf16)]
    first_slopes = call(
        functools.partial(slope_kernel, width=width),
        "slopes",
        slope_shapes,
        (source, gram, *proj),
        cost=cost,
    )
    generated, piece, flat, *slopes = call(
        functools.partial(second_kernel, width=width),
        "score",
        [
            latent_shape,
            latent_shape,
            shape((1, tokens), f32),
            *slope_shapes,
        ],
        (even, by1, mix, gram, *proj, readout, columns),
    )
    fake, adversarial, real = (swap(piece, "role", roles, bit) for bit in (2, 3, 1))
    flat, drawn = lax.optimization_barrier((flat, drawn))

    tail = (*first_slopes, *slopes, columns)
    cot, *send = call(
        send_kernel,
        "cotangent_send",
        [shape((2 * channels, tokens), bf16)] + [shape((rows, tile), bf16)] * chains,
        (real, adversarial, fake, generated, piece, flat, *tail),
        cost=cost,
    )
    kept = call(
        keep_kernel, "cotangent_keep", [shape((rows, tile), f32)] * chains, (cot, *tail), cost=cost
    )
    totals, others = add_all(kept, send, n)
    factor = 1.0 / math.sqrt(tokens * n)
    grads = gradient(own_rows, totals, 0, factor, cols)
    for at, other in enumerate(others, chains):
        grads = gradient(own_rows, [other], at, factor, cols, grads)
    return (grads, drawn.T)


def solution(mesh):
    in_specs = (
        P("fsdp", None),
        P("fsdp", None),
        P("fsdp"),
        P("role", None, None),
        P("role", None),
        P("role", None),
        P("role", "fsdp", None),
        P("role", None, None),
    )
    out_specs = (P("role", "fsdp", None), P("fsdp", None))
    return jax.shard_map(shards, mesh=mesh, in_specs=in_specs, out_specs=out_specs, check_vma=False)
```

```python
import functools
import math

import jax
import jax.numpy as jnp
from jax import lax
from jax.experimental import pallas as pl
from jax.experimental.pallas import tpu as pltpu
from jax.sharding import PartitionSpec as P

adv_weight = 3.0
f32 = jnp.float32
bf16 = jnp.bfloat16
extra = 8
chains = 2
part_limit = 54528
curve = math.sqrt(2.0 / math.pi)
bend = 0.044715


def halves(value):
    high = value.astype(bf16)
    return high, (value - high.astype(f32)).astype(bf16)


def mm(left, right, left_dim, right_dim):
    return lax.dot_general(
        left, right, (((left_dim,), (right_dim,)), ((), ())), preferred_element_type=f32
    )


def gelu_gate(hidden):
    square = hidden * hidden
    return 0.5 + 0.5 * jnp.tanh(hidden * (curve + (curve * bend) * square)), square


def gelu_slope(hidden, square, gate):
    return gate + (gate - gate * gate) * (hidden * (2.0 * curve + (6.0 * curve * bend) * square))


def level_rows(level):
    high = level.astype(bf16).astype(f32)
    mid = (level - high).astype(bf16).astype(f32)
    low = (level - high - mid).astype(bf16).astype(f32)
    row = lax.broadcasted_iota(jnp.int32, (extra, level.shape[1]), 0)
    return jnp.where(row == 0, high, jnp.where(row == 1, mid, jnp.where(row == 2, low, 0.0)))


def widen(latent, level):
    return jnp.concatenate([latent.astype(f32), level_rows(level)], axis=0)


def norm_scale(wide, gram, width):
    seen = lax.dot_general(
        gram,
        wide,
        (((1,), (0,)), ((), ())),
        precision=lax.Precision.HIGHEST,
        preferred_element_type=f32,
    )
    square = jnp.sum(seen * wide, axis=0, keepdims=True)
    return lax.rsqrt(square * (1.0 / width) + 1e-06), seen


def columns_of(at, tile):
    kept = lax.axis_index("fsdp") & 1
    base = tile * ((at % chains) + chains * (kept if at < chains else 1 - kept))
    return pl.ds(pl.multiple_of(base, tile), tile)


def part_kernel(embed_ref, vectors_ref, block_ref, *rest):
    *outs, embed, buffer, sems = rest
    place = lax.axis_index("fsdp")
    depth, cols = buffer.shape
    tile = cols // (2 * chains)
    own = slice(None)
    if embed_ref.shape[1] != depth:
        own = pl.ds(pl.multiple_of(place * depth, depth), depth)
    small = pltpu.make_async_copy(embed_ref.at[:, own], embed, sems.at[2 * chains])
    order = [*range(chains, 2 * chains), *range(chains)]
    large = [
        pltpu.make_async_copy(
            block_ref.at[0, :, columns_of(at, tile)],
            buffer.at[:, at * tile : (at + 1) * tile],
            sems.at[at],
        )
        for at in order
    ]
    small.start()
    for copy in large:
        copy.start()
    stamp, gain = vectors_ref[0:1, own], vectors_ref[1:2, own]
    row = lax.broadcasted_iota(jnp.int32, (extra, depth), 0)
    stamped = jnp.where(row < 3, stamp * gain, 0.0)
    small.wait()
    gained = jnp.concatenate([embed[...].astype(f32) * gain, stamped], axis=0)
    rows = gained.shape[0]
    both = jnp.concatenate([gained, gained - gained.astype(bf16).astype(f32)], axis=0).astype(bf16)
    outs[2 * chains][...] = both
    for at, copy in zip(order, large):
        copy.wait()
        part = mm(both, buffer[:, at * tile : (at + 1) * tile], 1, 0)
        outs[at][...] = (part[:rows] + part[rows:]).astype(outs[at].dtype)


def network(wide16, scale, proj_refs, first_piece, readout_ref):
    tile = proj_refs[0].shape[1]
    total = jnp.zeros((readout_ref.shape[0], wide16.shape[1]), f32)
    for at, proj_ref in enumerate(proj_refs, first_piece):
        hidden = scale * mm(proj_ref[...], wide16, 0, 0)
        gate, unused = gelu_gate(hidden)
        activated = (hidden * gate).astype(bf16)
        total = total + mm(readout_ref[:, columns_of(at, tile)], activated, 1, 0)
    return total


def network_by_rows(wide, scale, turned_ref, tile, readout_ref, slope_ref):
    total = jnp.zeros((readout_ref.shape[0], wide.shape[1]), f32)
    wide16 = lanes_of_zeros(wide).astype(bf16)
    for at in range(2 * chains):
        rows = slice(at * tile, (at + 1) * tile)
        hidden = scale * mm(turned_ref[rows, :], wide16, 1, 0)
        gate, square = gelu_gate(hidden)
        activated = (hidden * gate).astype(bf16)
        total = total + mm(readout_ref[:, columns_of(at, tile)], activated, 1, 0)
        slope_ref[rows, :] = gelu_slope(hidden, square, gate)
    return total


def lanes_of_zeros(wide, lanes=128):
    return jnp.concatenate([wide, jnp.zeros((lanes - wide.shape[0], wide.shape[1]), f32)], axis=0)


def early_kernel(latent_ref, gram_ref, *rest, width):
    *proj_refs, readout_ref, total_ref = rest
    channels, tokens = latent_ref.shape

    @pl.when(lax.axis_index("role") == 0)
    def _():
        wide = widen(latent_ref[...], jnp.ones((1, tokens), f32))
        scale, unused = norm_scale(wide, gram_ref[...], width)
        total_ref[:channels, :] = network(wide.astype(bf16), scale, proj_refs, 0, readout_ref)
        total_ref[channels:, :] = jnp.broadcast_to(scale, (extra, tokens))


def late_kernel(latent_ref, noise_ref, level_ref, gram_ref, total_ref, *rest):
    *proj_refs, readout_ref, out_ref, mix_ref, gram_out_ref = rest
    channels, tokens = latent_ref.shape
    level = level_ref[...]
    mix_ref[:channels, :] = level * noise_ref[...].astype(f32)
    mix_ref[channels:, :] = jnp.broadcast_to(level, (extra, tokens))
    gram_out_ref[...] = gram_ref[...]

    @pl.when(lax.axis_index("role") == 0)
    def _():
        wide16 = widen(latent_ref[...], jnp.ones((1, tokens), f32)).astype(bf16)
        scale = total_ref[channels : channels + 1, :]
        total = network(wide16, scale, proj_refs, chains, readout_ref)
        out_ref[...] = (total_ref[:channels, :] + total).astype(bf16)


def in_parts(scale, wide):
    scaled = scale * wide
    return jnp.concatenate([scaled, scaled - scaled.astype(bf16).astype(f32)], axis=0).astype(bf16)


def slope_kernel(latent_ref, gram_ref, own_ref, *rest, width):
    *proj_refs, own_turned_ref, turned_ref, slope_ref, scaled_ref = rest
    own_turned_ref[...] = lanes_of_zeros(own_ref[...].astype(f32), 256).T.astype(bf16)
    tile = proj_refs[0].shape[1]
    for at, proj_ref in enumerate(proj_refs):
        turned = lanes_of_zeros(proj_ref[...].astype(f32)).T
        turned_ref[at * tile : (at + 1) * tile, :] = turned.astype(bf16)

    @pl.when(lax.axis_index("role") == 0)
    def _():
        wide = widen(latent_ref[...], jnp.ones((1, latent_ref.shape[1]), f32))
        scale, unused = norm_scale(wide, gram_ref[...], width)
        wide16 = lanes_of_zeros(wide).astype(bf16)
        for at in range(2 * chains):
            hidden = scale * mm(turned_ref[at * tile : (at + 1) * tile, :], wide16, 1, 0)
            gate, square = gelu_gate(hidden)
            slope_ref[at * tile : (at + 1) * tile, :] = gelu_slope(hidden, square, gate)
        scaled_ref[...] = in_parts(scale, wide)


def second_kernel(own_ref, by2_ref, by3_ref, by1_ref, mix_ref, gram_ref, *rest, width):
    proj_refs = rest[: 2 * chains]
    turned_ref, readout_ref, columns_ref, generated_ref, piece_ref, flat_ref, slope_ref, scaled_ref = rest[2 * chains :]
    role = lax.axis_index("role")
    channels, tokens = own_ref.shape
    tile = proj_refs[0].shape[1]
    low = jnp.where(role == 0, own_ref[...].astype(f32), by1_ref[...].astype(f32))
    high = jnp.where(role == 2, by2_ref[...].astype(f32), by3_ref[...].astype(f32))
    generated = jnp.where(role < 2, low, high)
    generated_ref[...] = generated.astype(bf16)

    @pl.when(role > 0)
    def _():
        level = mix_ref[channels : channels + 1, :]
        noised = (1.0 - level) * generated + mix_ref[:channels, :]
        wide = widen(noised.astype(bf16), level)
        scale, seen = norm_scale(wide, gram_ref[...], width)
        scores = network_by_rows(wide, scale, turned_ref, tile, readout_ref, slope_ref).astype(bf16)
        piece_ref[...] = scores
        logit = jnp.sum(scores.astype(f32), axis=0, keepdims=True)
        flat_ref[...] = 1.0 / (1.0 + jnp.exp(-logit))
        scaled_ref[...] = in_parts(scale, wide)

        @pl.when(role == 3)
        def _():
            high, low = halves(-1.0 / (1.0 + jnp.exp(logit)))
            cot = jnp.concatenate(
                [
                    jnp.broadcast_to(high, (channels, tokens)),
                    jnp.broadcast_to(low, (channels, tokens)),
                ],
                axis=0,
            )
            back_rows = jnp.zeros(wide.shape, f32)
            for at, proj_ref in enumerate(proj_refs):
                back = mm(columns_ref[columns_of(at, tile), :], cot, 1, 0)
                hcot = (back * slope_ref[at * tile : (at + 1) * tile, :]).astype(bf16)
                back_rows = back_rows + mm(proj_ref[...], hcot, 1, 0)
            inner = scale * jnp.sum(back_rows * wide, axis=0, keepdims=True)
            latent_back = scale * back_rows[:channels] - (scale * scale * inner * (1.0 / width)) * seen[:channels]
            piece_ref[...] = (adv_weight * (1.0 - level) * latent_back).astype(bf16)


def pull_back(cot, tail, out_refs, first_piece):
    first = lax.axis_index("role") == 0
    rows, tile = out_refs[0].shape
    columns_ref = tail[4]

    def with_slopes(slope_ref, scaled_ref):
        scaled = scaled_ref[...]
        for at, out_ref in enumerate(out_refs, first_piece):
            back = mm(columns_ref[columns_of(at, tile), :], cot, 1, 0)
            hcot = (back * slope_ref[at * tile : (at + 1) * tile, :]).astype(bf16)
            part = mm(scaled, hcot, 1, 1)
            out_ref[...] = (part[:rows] + part[rows:]).astype(out_ref.dtype)

    pl.when(first)(lambda: with_slopes(*tail[0:2]))
    pl.when(jnp.logical_not(first))(lambda: with_slopes(*tail[2:4]))


def send_kernel(
    fake_ref,
    adversarial_ref,
    real_ref,
    generated_ref,
    piece_ref,
    flat_ref,
    *rest,
):
    tail, cot_ref, out_refs = rest[:5], rest[5], rest[6:]
    role = lax.axis_index("role")
    first = role == 0
    generated = generated_ref[...].astype(f32)
    piece = piece_ref[...].astype(f32)
    fake = fake_ref[...].astype(f32)
    real = real_ref[...].astype(f32)
    adversarial = adversarial_ref[...].astype(f32)
    spread = jnp.mean(jnp.abs(generated - real), axis=0, keepdims=True) + 1e-05
    dmd = (fake - real) / spread
    flat = jnp.broadcast_to(flat_ref[...], generated.shape)
    flat_high = flat.astype(bf16).astype(f32)
    left = jnp.where(
        first, dmd, jnp.where(role == 2, piece, jnp.where(role == 3, flat_high, 0.0))
    ).astype(bf16)
    right = jnp.where(
        first,
        adversarial,
        jnp.where(role == 2, -generated, jnp.where(role == 3, flat - flat_high, 0.0)),
    ).astype(bf16)
    cot = jnp.concatenate([left, right], axis=0)
    cot_ref[...] = cot
    pull_back(cot, tail, out_refs, chains)


def keep_kernel(cot_ref, *rest):
    pull_back(cot_ref[...], rest[:5], rest[5:], 0)


def grad_kernel(own_ref, *rest, factor, first_piece, count):
    total_refs = rest[:count]
    *unused, out_ref, buffer, sems = rest[count:]
    tile = buffer.shape[1] // count
    own = own_ref[...]
    copies = []
    for at, total_ref in enumerate(total_refs):
        here = slice(at * tile, (at + 1) * tile)
        total = total_ref[...].astype(f32)
        part = mm(own, lanes_of_zeros(jnp.concatenate([total, total], axis=0), 256).astype(bf16), 1, 0)
        buffer[:, here] = part * factor
        cols = columns_of(first_piece + at, tile)
        copy = pltpu.make_async_copy(buffer.at[:, here], out_ref.at[0, :, cols], sems.at[at])
        copy.start()
        copies.append(copy)
    for copy in copies:
        copy.wait()


def call(kernel, name, out_shape, inputs, scratch=(), cost=0):
    many = isinstance(out_shape, list)
    vmem = pl.BlockSpec(memory_space=pltpu.VMEM)
    return pl.pallas_call(
        kernel,
        out_shape=out_shape,
        in_specs=[vmem] * len(inputs),
        out_specs=[vmem] * len(out_shape) if many else vmem,
        scratch_shapes=list(scratch),
        compiler_params=pltpu.CompilerParams(vmem_limit_bytes=16 * 1024 * 1024),
        cost_estimate=pl.CostEstimate(flops=cost, bytes_accessed=cost // 1000, transcendentals=cost // 1000),
        name=name,
    )(*inputs)


def part_of(embed_w, vectors, block_weight):
    depth, cols = block_weight.shape[1:]
    channels = embed_w.shape[0]
    rows, tile = channels + extra, cols // (2 * chains)
    if depth % 128 != 0:
        embed_w, vectors = (
            lax.dynamic_slice_in_dim(value, lax.axis_index("fsdp") * depth, depth, 1)
            for value in (embed_w, vectors)
        )
    shapes = [jax.ShapeDtypeStruct((rows, tile), dtype) for dtype in (f32, bf16) for at in range(chains)]
    shapes.append(jax.ShapeDtypeStruct((2 * rows, depth), bf16))
    vmem = pl.BlockSpec(memory_space=pltpu.VMEM)
    hbm = pl.BlockSpec(memory_space=pltpu.HBM)
    return pl.pallas_call(
        part_kernel,
        out_shape=shapes,
        in_specs=[hbm, vmem, hbm],
        out_specs=[vmem] * len(shapes),
        scratch_shapes=[
            pltpu.VMEM((channels, depth), bf16),
            pltpu.VMEM((depth, cols), bf16),
            pltpu.SemaphoreType.DMA((2 * chains + 1,)),
        ],
        compiler_params=pltpu.CompilerParams(vmem_limit_bytes=part_limit * 1024),
        cost_estimate=pl.CostEstimate(
            flops=4 * rows * depth * cols, bytes_accessed=2 * depth * cols, transcendentals=0
        ),
        name="part",
    )(embed_w, vectors, block_weight)


def gradient(own, totals, first_piece, factor, cols, buffer=None):
    depth, tile, count = own.shape[0], cols // (2 * chains), len(totals)
    vmem = pl.BlockSpec(memory_space=pltpu.VMEM)
    hbm = pl.BlockSpec(memory_space=pltpu.HBM)
    specs = [vmem] * (1 + count)
    inputs = [own, *totals]
    if buffer is not None:
        specs.append(hbm)
        inputs.append(buffer)
    return pl.pallas_call(
        functools.partial(grad_kernel, factor=factor, first_piece=first_piece, count=count),
        out_shape=jax.ShapeDtypeStruct((1, depth, cols), f32),
        in_specs=specs,
        out_specs=hbm,
        input_output_aliases={} if buffer is None else {len(inputs) - 1: 0},
        scratch_shapes=[pltpu.VMEM((depth, count * tile), f32), pltpu.SemaphoreType.DMA((count,))],
        compiler_params=pltpu.CompilerParams(vmem_limit_bytes=16 * 1024 * 1024),
        cost_estimate=pl.CostEstimate(
            flops=2 * own.shape[1] * depth * count * tile,
            bytes_accessed=4 * depth * count * tile,
            transcendentals=0,
        ),
        name="gradient",
    )(*inputs)


def swap(value, axis, n, bit):
    return lax.ppermute(value, axis, [(i, i ^ bit) for i in range(n)])


def add_all(kept, sent, n):
    bits = [1 << at for at in range(n.bit_length() - 1)]
    mine = []
    for value, part in zip(kept, sent):
        for bit in bits:
            outgoing = part if bit == 1 else value.astype(bf16)
            value = value + swap(outgoing, "fsdp", n, bit).astype(f32)
        mine.append(value.astype(bf16))
    return mine, [swap(value, "fsdp", n, 1) for value in mine]


def shards(
    source_noise,
    score_noise,
    noise_level,
    embed_weight,
    time_vector,
    norm_gain,
    block_weight,
    readout_weight,
):
    role = lax.axis_index("role")
    n = lax.axis_size("fsdp")
    embed_w = embed_weight[0]
    readout = readout_weight[0].T
    depth, cols = block_weight.shape[1:]
    channels, width = embed_w.shape
    tokens = source_noise.shape[0]
    rows = channels + extra
    tile = cols // (2 * chains)
    shape = jax.ShapeDtypeStruct
    roles = lax.axis_size("role")

    vectors = jnp.concatenate([time_vector, norm_gain], axis=0)
    *parts, own_rows = part_of(embed_w, vectors, block_weight)
    mine, others = add_all(parts[:chains], parts[chains:], n)
    proj = mine + others

    tall = jnp.concatenate(
        [embed_w.astype(f32), jnp.broadcast_to(time_vector, (3, width)), jnp.zeros((extra - 3, width), f32)]
    )
    gram = jnp.dot(tall, tall.T, precision=lax.Precision.HIGHEST)
    columns = jnp.concatenate([readout, readout], axis=0).T
    level = noise_level[None, :]
    source = source_noise.T
    latent_shape = shape((channels, tokens), bf16)

    cost = 2 * rows * tokens * cols
    total = call(
        functools.partial(early_kernel, width=width),
        "generator_early",
        shape((rows, tokens), f32),
        (source, gram, *mine, readout),
        cost=cost,
    )
    own_first, mix, gram = call(
        late_kernel,
        "generator_late",
        [latent_shape, shape((rows, tokens), f32), shape((rows, rows), f32)],
        (source, score_noise.T, level, gram, total, *others, readout),
    )
    by2, by3, by1 = (swap(own_first, "role", roles, bit) for bit in (2, 3, 1))
    drawn = jnp.where(role == 0, own_first, jnp.where(role == 1, by1, jnp.where(role == 2, by2, by3)))
    slope_shapes = [shape((cols, tokens), f32), shape((2 * rows, tokens), bf16)]
    own_turned, turned, *first_slopes = call(
        functools.partial(slope_kernel, width=width),
        "slopes",
        [shape((depth, 256), bf16), shape((cols, 128), bf16), *slope_shapes],
        (source, gram, own_rows, *proj),
        cost=cost,
    )
    generated, piece, flat, *slopes = call(
        functools.partial(second_kernel, width=width),
        "score",
        [
            latent_shape,
            latent_shape,
            shape((1, tokens), f32),
            *slope_shapes,
        ],
        (own_first, by2, by3, by1, mix, gram, *proj, turned, readout, columns),
    )
    fake, adversarial, real = (swap(piece, "role", roles, bit) for bit in (2, 3, 1))
    flat, drawn = lax.optimization_barrier((flat, drawn))

    tail = (*first_slopes, *slopes, columns)
    cot, *send = call(
        send_kernel,
        "cotangent_send",
        [shape((2 * channels, tokens), bf16)] + [shape((rows, tile), bf16)] * chains,
        (fake, adversarial, real, generated, piece, flat, *tail),
        cost=cost,
    )
    kept = call(
        keep_kernel, "cotangent_keep", [shape((rows, tile), f32)] * chains, (cot, *tail), cost=cost
    )
    totals, others = add_all(kept, send, n)
    factor = 1.0 / math.sqrt(tokens * n)
    grads = gradient(own_turned, totals, 0, factor, cols)
    for at, other in enumerate(others, chains):
        grads = gradient(own_turned, [other], at, factor, cols, grads)
    return (grads, drawn.T)


def solution(mesh):
    in_specs = (
        P("fsdp", None),
        P("fsdp", None),
        P("fsdp"),
        P("role", None, None),
        P("role", None),
        P("role", None),
        P("role", "fsdp", None),
        P("role", None, None),
    )
    out_specs = (P("role", "fsdp", None), P("fsdp", None))
    return jax.shard_map(shards, mesh=mesh, in_specs=in_specs, out_specs=out_specs, check_vma=False)
```

```python
import functools
import math

import jax
import jax.numpy as jnp
from jax import lax
from jax.experimental import pallas as pl
from jax.experimental.pallas import tpu as pltpu
from jax.sharding import PartitionSpec as P

adv_weight = 3.0
f32 = jnp.float32
bf16 = jnp.bfloat16
extra = 8
chains = 2
part_limit = 54528
curve = math.sqrt(2.0 / math.pi)
bend = 0.044715


def halves(value):
    high = value.astype(bf16)
    return high, (value - high.astype(f32)).astype(bf16)


def mm(left, right, left_dim, right_dim):
    return lax.dot_general(
        left, right, (((left_dim,), (right_dim,)), ((), ())), preferred_element_type=f32
    )


def gelu_gate(hidden):
    square = hidden * hidden
    return 0.5 + 0.5 * jnp.tanh(hidden * (curve + (curve * bend) * square)), square


def gelu_slope(hidden, square, gate):
    return gate + (gate - gate * gate) * (hidden * (2.0 * curve + (6.0 * curve * bend) * square))


def level_rows(level):
    high = level.astype(bf16).astype(f32)
    mid = (level - high).astype(bf16).astype(f32)
    low = (level - high - mid).astype(bf16).astype(f32)
    row = lax.broadcasted_iota(jnp.int32, (extra, level.shape[1]), 0)
    return jnp.where(row == 0, high, jnp.where(row == 1, mid, jnp.where(row == 2, low, 0.0)))


def widen(latent, level):
    return jnp.concatenate([latent.astype(f32), level_rows(level)], axis=0)


def norm_scale(wide, gram, width):
    seen = lax.dot_general(
        gram,
        wide,
        (((1,), (0,)), ((), ())),
        precision=lax.Precision.HIGHEST,
        preferred_element_type=f32,
    )
    square = jnp.sum(seen * wide, axis=0, keepdims=True)
    return lax.rsqrt(square * (1.0 / width) + 1e-06), seen


def columns_of(at, tile):
    kept = lax.axis_index("fsdp") & 1
    base = tile * ((at % chains) + chains * (kept if at < chains else 1 - kept))
    return pl.ds(pl.multiple_of(base, tile), tile)


def part_kernel(embed_ref, vectors_ref, block_ref, *rest):
    *outs, embed, buffer, sems = rest
    place = lax.axis_index("fsdp")
    depth, cols = buffer.shape
    tile = cols // (2 * chains)
    own = slice(None)
    if embed_ref.shape[1] != depth:
        own = pl.ds(pl.multiple_of(place * depth, depth), depth)
    small = pltpu.make_async_copy(embed_ref.at[:, own], embed, sems.at[2 * chains])
    order = [*range(chains, 2 * chains), *range(chains)]
    large = [
        pltpu.make_async_copy(
            block_ref.at[0, :, columns_of(at, tile)],
            buffer.at[:, at * tile : (at + 1) * tile],
            sems.at[at],
        )
        for at in order
    ]
    small.start()
    for copy in large:
        copy.start()
    stamp, gain = vectors_ref[0:1, own], vectors_ref[1:2, own]
    row = lax.broadcasted_iota(jnp.int32, (extra, depth), 0)
    stamped = jnp.where(row < 3, stamp * gain, 0.0)
    small.wait()
    gained = jnp.concatenate([embed[...].astype(f32) * gain, stamped], axis=0)
    rows = gained.shape[0]
    both = jnp.concatenate([gained, gained - gained.astype(bf16).astype(f32)], axis=0).astype(bf16)
    outs[2 * chains][...] = both
    for at, copy in zip(order, large):
        copy.wait()
        part = mm(both, buffer[:, at * tile : (at + 1) * tile], 1, 0)
        outs[at][...] = (part[:rows] + part[rows:]).astype(outs[at].dtype)


def network(wide16, scale, proj_refs, first_piece, readout_ref, slope_ref=None):
    tile = proj_refs[0].shape[1]
    total = jnp.zeros((readout_ref.shape[0], wide16.shape[1]), f32)
    for at, proj_ref in enumerate(proj_refs, first_piece):
        hidden = scale * mm(proj_ref[...], wide16, 0, 0)
        gate, square = gelu_gate(hidden)
        activated = (hidden * gate).astype(bf16)
        total = total + mm(readout_ref[:, columns_of(at, tile)], activated, 1, 0)
        if slope_ref is not None:
            slope_ref[at * tile : (at + 1) * tile, :] = gelu_slope(hidden, square, gate)
    return total


def lanes_of_zeros(wide, lanes=128):
    return jnp.concatenate([wide, jnp.zeros((lanes - wide.shape[0], wide.shape[1]), f32)], axis=0)


def early_kernel(latent_ref, gram_ref, *rest, width):
    *proj_refs, readout_ref, total_ref = rest
    channels, tokens = latent_ref.shape

    @pl.when(lax.axis_index("role") == 0)
    def _():
        wide = widen(latent_ref[...], jnp.ones((1, tokens), f32))
        scale, unused = norm_scale(wide, gram_ref[...], width)
        total_ref[:channels, :] = network(wide.astype(bf16), scale, proj_refs, 0, readout_ref)
        total_ref[channels:, :] = jnp.broadcast_to(scale, (extra, tokens))


def late_kernel(latent_ref, noise_ref, level_ref, gram_ref, total_ref, *rest):
    *proj_refs, readout_ref, out_ref, mix_ref, gram_out_ref = rest
    channels, tokens = latent_ref.shape
    level = level_ref[...]
    mix_ref[:channels, :] = level * noise_ref[...].astype(f32)
    mix_ref[channels:, :] = jnp.broadcast_to(level, (extra, tokens))
    gram_out_ref[...] = gram_ref[...]

    @pl.when(lax.axis_index("role") == 0)
    def _():
        wide16 = widen(latent_ref[...], jnp.ones((1, tokens), f32)).astype(bf16)
        scale = total_ref[channels : channels + 1, :]
        total = network(wide16, scale, proj_refs, chains, readout_ref)
        out_ref[...] = (total_ref[:channels, :] + total).astype(bf16)


def slope_kernel(latent_ref, scaled_in_ref, gram_ref, own_ref, *rest, width):
    *proj_refs, own_turned_ref, slope_ref, scaled_ref = rest
    own_turned_ref[...] = lanes_of_zeros(own_ref[...].astype(f32), 256).T.astype(bf16)
    rows, tile = proj_refs[0].shape
    wide = widen(latent_ref[...], jnp.ones((1, latent_ref.shape[1]), f32))
    scale, unused = norm_scale(wide, gram_ref[...], width)
    scaled = jnp.where(lax.axis_index("role") == 0, scale * wide, scaled_in_ref[...])
    high, low = halves(scaled)
    scaled_ref[...] = jnp.concatenate([scaled, scaled - high.astype(f32)], axis=0).astype(bf16)
    for at, proj_ref in enumerate(proj_refs):
        hidden = mm(proj_ref[...], high, 0, 0) + mm(proj_ref[...], low, 0, 0)
        gate, square = gelu_gate(hidden)
        slope_ref[at * tile : (at + 1) * tile, :] = gelu_slope(hidden, square, gate)


def second_kernel(own_ref, by1_ref, by3_ref, by2_ref, mix_ref, gram_ref, *rest, width):
    proj_refs = rest[: 2 * chains]
    readout_ref, columns_ref, generated_ref, piece_ref, flat_ref, scaled_ref, slope_ref = rest[2 * chains :]
    role = lax.axis_index("role")
    channels, tokens = own_ref.shape
    tile = proj_refs[0].shape[1]
    low = jnp.where(role == 0, own_ref[...].astype(f32), by1_ref[...].astype(f32))
    high = jnp.where(role == 2, by2_ref[...].astype(f32), by3_ref[...].astype(f32))
    generated = jnp.where(role < 2, low, high)
    generated_ref[...] = generated.astype(bf16)

    def score(slope_ref):
        level = mix_ref[channels : channels + 1, :]
        noised = (1.0 - level) * generated + mix_ref[:channels, :]
        wide = widen(noised.astype(bf16), level)
        scale, seen = norm_scale(wide, gram_ref[...], width)
        scaled_ref[...] = scale * wide
        scores = network(wide.astype(bf16), scale, proj_refs, 0, readout_ref, slope_ref).astype(bf16)
        return level, wide, scale, seen, scores

    @pl.when((role == 1) | (role == 2))
    def _():
        piece_ref[...] = score(None)[4]

    @pl.when(role == 3)
    def _():
        level, wide, scale, seen, scores = score(slope_ref)
        logit = jnp.sum(scores.astype(f32), axis=0, keepdims=True)
        flat_ref[...] = 1.0 / (1.0 + jnp.exp(-logit))
        high, low = halves(-1.0 / (1.0 + jnp.exp(logit)))
        cot = jnp.concatenate(
            [
                jnp.broadcast_to(high, (channels, tokens)),
                jnp.broadcast_to(low, (channels, tokens)),
            ],
            axis=0,
        )
        back_rows = jnp.zeros(wide.shape, f32)
        for at, proj_ref in enumerate(proj_refs):
            back = mm(columns_ref[columns_of(at, tile), :], cot, 1, 0)
            hcot = (back * slope_ref[at * tile : (at + 1) * tile, :]).astype(bf16)
            back_rows = back_rows + mm(proj_ref[...], hcot, 1, 0)
        inner = scale * jnp.sum(back_rows * wide, axis=0, keepdims=True)
        latent_back = scale * back_rows[:channels] - (scale * scale * inner * (1.0 / width)) * seen[:channels]
        piece_ref[...] = (adv_weight * (1.0 - level) * latent_back).astype(bf16)


def pull_back(cot, tail, out_refs, first_piece):
    slope_ref, scaled_ref, columns_ref = tail
    rows, tile = out_refs[0].shape
    scaled = scaled_ref[...]
    for at, out_ref in enumerate(out_refs, first_piece):
        back = mm(columns_ref[columns_of(at, tile), :], cot, 1, 0)
        hcot = (back * slope_ref[at * tile : (at + 1) * tile, :]).astype(bf16)
        part = mm(scaled, hcot, 1, 1)
        out_ref[...] = (part[:rows] + part[rows:]).astype(out_ref.dtype)


def send_kernel(
    real_ref,
    adversarial_ref,
    fake_ref,
    generated_ref,
    piece_ref,
    flat_ref,
    *rest,
):
    tail, cot_ref, out_refs = rest[:3], rest[3], rest[4:]
    role = lax.axis_index("role")
    first = role == 0
    generated = generated_ref[...].astype(f32)
    piece = piece_ref[...].astype(f32)
    fake = fake_ref[...].astype(f32)
    real = real_ref[...].astype(f32)
    adversarial = adversarial_ref[...].astype(f32)
    spread = jnp.mean(jnp.abs(generated - real), axis=0, keepdims=True) + 1e-05
    dmd = (fake - real) / spread
    flat = jnp.broadcast_to(flat_ref[...], generated.shape)
    flat_high = flat.astype(bf16).astype(f32)
    left = jnp.where(
        first, dmd, jnp.where(role == 2, piece, jnp.where(role == 3, flat_high, 0.0))
    ).astype(bf16)
    right = jnp.where(
        first,
        adversarial,
        jnp.where(role == 2, -generated, jnp.where(role == 3, flat - flat_high, 0.0)),
    ).astype(bf16)
    cot = jnp.concatenate([left, right], axis=0)
    cot_ref[...] = cot
    pull_back(cot, tail, out_refs, chains)


def keep_kernel(cot_ref, *rest):
    pull_back(cot_ref[...], rest[:3], rest[3:], 0)


def grad_kernel(own_ref, *rest, factor, first_piece, count):
    total_refs = rest[:count]
    *unused, out_ref, buffer, sems = rest[count:]
    tile = buffer.shape[1] // count
    own = own_ref[...]
    copies = []
    for at, total_ref in enumerate(total_refs):
        here = slice(at * tile, (at + 1) * tile)
        total = total_ref[...].astype(f32)
        part = mm(own, lanes_of_zeros(jnp.concatenate([total, total], axis=0), 256).astype(bf16), 1, 0)
        buffer[:, here] = part * factor
        cols = columns_of(first_piece + at, tile)
        copy = pltpu.make_async_copy(buffer.at[:, here], out_ref.at[0, :, cols], sems.at[at])
        copy.start()
        copies.append(copy)
    for copy in copies:
        copy.wait()


def call(kernel, name, out_shape, inputs, scratch=(), cost=0):
    many = isinstance(out_shape, list)
    vmem = pl.BlockSpec(memory_space=pltpu.VMEM)
    return pl.pallas_call(
        kernel,
        out_shape=out_shape,
        in_specs=[vmem] * len(inputs),
        out_specs=[vmem] * len(out_shape) if many else vmem,
        scratch_shapes=list(scratch),
        compiler_params=pltpu.CompilerParams(vmem_limit_bytes=16 * 1024 * 1024),
        cost_estimate=pl.CostEstimate(flops=cost, bytes_accessed=cost // 1000, transcendentals=cost // 1000),
        name=name,
    )(*inputs)


def part_of(embed_w, vectors, block_weight):
    depth, cols = block_weight.shape[1:]
    channels = embed_w.shape[0]
    rows, tile = channels + extra, cols // (2 * chains)
    if depth % 128 != 0:
        embed_w, vectors = (
            lax.dynamic_slice_in_dim(value, lax.axis_index("fsdp") * depth, depth, 1)
            for value in (embed_w, vectors)
        )
    shapes = [jax.ShapeDtypeStruct((rows, tile), dtype) for dtype in (f32, bf16) for at in range(chains)]
    shapes.append(jax.ShapeDtypeStruct((2 * rows, depth), bf16))
    vmem = pl.BlockSpec(memory_space=pltpu.VMEM)
    hbm = pl.BlockSpec(memory_space=pltpu.HBM)
    return pl.pallas_call(
        part_kernel,
        out_shape=shapes,
        in_specs=[hbm, vmem, hbm],
        out_specs=[vmem] * len(shapes),
        scratch_shapes=[
            pltpu.VMEM((channels, depth), bf16),
            pltpu.VMEM((depth, cols), bf16),
            pltpu.SemaphoreType.DMA((2 * chains + 1,)),
        ],
        compiler_params=pltpu.CompilerParams(vmem_limit_bytes=part_limit * 1024),
        cost_estimate=pl.CostEstimate(
            flops=4 * rows * depth * cols, bytes_accessed=2 * depth * cols, transcendentals=0
        ),
        name="part",
    )(embed_w, vectors, block_weight)


def gradient(own, totals, first_piece, factor, cols, buffer=None):
    depth, tile, count = own.shape[0], cols // (2 * chains), len(totals)
    vmem = pl.BlockSpec(memory_space=pltpu.VMEM)
    hbm = pl.BlockSpec(memory_space=pltpu.HBM)
    specs = [vmem] * (1 + count)
    inputs = [own, *totals]
    if buffer is not None:
        specs.append(hbm)
        inputs.append(buffer)
    return pl.pallas_call(
        functools.partial(grad_kernel, factor=factor, first_piece=first_piece, count=count),
        out_shape=jax.ShapeDtypeStruct((1, depth, cols), f32),
        in_specs=specs,
        out_specs=hbm,
        input_output_aliases={} if buffer is None else {len(inputs) - 1: 0},
        scratch_shapes=[pltpu.VMEM((depth, count * tile), f32), pltpu.SemaphoreType.DMA((count,))],
        compiler_params=pltpu.CompilerParams(vmem_limit_bytes=16 * 1024 * 1024),
        cost_estimate=pl.CostEstimate(
            flops=2 * own.shape[1] * depth * count * tile,
            bytes_accessed=4 * depth * count * tile,
            transcendentals=0,
        ),
        name="gradient",
    )(*inputs)


def swap(value, axis, n, bit):
    return lax.ppermute(value, axis, [(i, i ^ bit) for i in range(n)])


def add_all(kept, sent, n):
    bits = [1 << at for at in range(n.bit_length() - 1)]
    mine = []
    for value, part in zip(kept, sent):
        for bit in bits:
            outgoing = part if bit == 1 else value.astype(bf16)
            value = value + swap(outgoing, "fsdp", n, bit).astype(f32)
        mine.append(value.astype(bf16))
    return mine, [swap(value, "fsdp", n, 1) for value in mine]


def shards(
    source_noise,
    score_noise,
    noise_level,
    embed_weight,
    time_vector,
    norm_gain,
    block_weight,
    readout_weight,
):
    role = lax.axis_index("role")
    n = lax.axis_size("fsdp")
    embed_w = embed_weight[0]
    readout = readout_weight[0].T
    depth, cols = block_weight.shape[1:]
    channels, width = embed_w.shape
    tokens = source_noise.shape[0]
    rows = channels + extra
    tile = cols // (2 * chains)
    shape = jax.ShapeDtypeStruct
    roles = lax.axis_size("role")

    vectors = jnp.concatenate([time_vector, norm_gain], axis=0)
    *parts, own_rows = part_of(embed_w, vectors, block_weight)
    mine, others = add_all(parts[:chains], parts[chains:], n)
    proj = mine + others

    tall = jnp.concatenate(
        [embed_w.astype(f32), jnp.broadcast_to(time_vector, (3, width)), jnp.zeros((extra - 3, width), f32)]
    )
    gram = jnp.dot(tall, tall.T, precision=lax.Precision.HIGHEST)
    columns = jnp.concatenate([readout, readout], axis=0).T
    level = noise_level[None, :]
    source = source_noise.T
    latent_shape = shape((channels, tokens), bf16)

    cost = 2 * rows * tokens * cols
    total = call(
        functools.partial(early_kernel, width=width),
        "generator_early",
        shape((rows, tokens), f32),
        (source, gram, *mine, readout),
        cost=cost,
    )
    own_first, mix, gram = call(
        late_kernel,
        "generator_late",
        [latent_shape, shape((rows, tokens), f32), shape((rows, rows), f32)],
        (source, score_noise.T, level, gram, total, *others, readout),
    )
    by2, by3, by1 = (swap(own_first, "role", roles, bit) for bit in (2, 3, 1))
    drawn = jnp.where(role == 0, own_first, jnp.where(role == 1, by1, jnp.where(role == 2, by2, by3)))
    generated, piece, flat, scaled = call(
        functools.partial(second_kernel, width=width),
        "score",
        [latent_shape, latent_shape, shape((1, tokens), f32), shape((rows, tokens), f32)],
        (own_first, by1, by3, by2, mix, gram, *proj, readout, columns),
        scratch=[pltpu.VMEM((cols, tokens), f32)],
    )
    fake, adversarial, real = (swap(piece, "role", roles, bit) for bit in (2, 3, 1))
    own_turned, slope, scaled = call(
        functools.partial(slope_kernel, width=width),
        "slopes",
        [shape((depth, 256), bf16), shape((cols, tokens), f32), shape((2 * rows, tokens), bf16)],
        (source, scaled, gram, own_rows, *proj),
        cost=cost,
    )
    flat, drawn = lax.optimization_barrier((flat, drawn))

    tail = (slope, scaled, columns)
    cot, *send = call(
        send_kernel,
        "cotangent_send",
        [shape((2 * channels, tokens), bf16)] + [shape((rows, tile), bf16)] * chains,
        (real, adversarial, fake, generated, piece, flat, *tail),
        cost=cost,
    )
    kept = call(
        keep_kernel, "cotangent_keep", [shape((rows, tile), f32)] * chains, (cot, *tail), cost=cost
    )
    totals, others = add_all(kept, send, n)
    factor = 1.0 / math.sqrt(tokens * n)
    grads = gradient(own_turned, totals, 0, factor, cols)
    for at, other in enumerate(others, chains):
        grads = gradient(own_turned, [other], at, factor, cols, grads)
    return (grads, drawn.T)


def solution(mesh):
    in_specs = (
        P("fsdp", None),
        P("fsdp", None),
        P("fsdp"),
        P("role", None, None),
        P("role", None),
        P("role", None),
        P("role", "fsdp", None),
        P("role", None, None),
    )
    out_specs = (P("role", "fsdp", None), P("fsdp", None))
    return jax.shard_map(shards, mesh=mesh, in_specs=in_specs, out_specs=out_specs, check_vma=False)
```

```python
import functools
import math

import jax
import jax.numpy as jnp
from jax import lax
from jax.experimental import pallas as pl
from jax.experimental.pallas import tpu as pltpu
from jax.sharding import PartitionSpec as P

adv_weight = 3.0
f32 = jnp.float32
bf16 = jnp.bfloat16
extra = 8
chains = 2
part_limit = 54528
curve = math.sqrt(2.0 / math.pi)
bend = 0.044715


def halves(value):
    high = value.astype(bf16)
    return high, (value - high.astype(f32)).astype(bf16)


def mm(left, right, left_dim, right_dim):
    return lax.dot_general(
        left, right, (((left_dim,), (right_dim,)), ((), ())), preferred_element_type=f32
    )


def gelu_gate(hidden):
    square = hidden * hidden
    return 0.5 + 0.5 * jnp.tanh(hidden * (curve + (curve * bend) * square)), square


def gelu_slope(hidden, square, gate):
    return gate + (gate - gate * gate) * (hidden * (2.0 * curve + (6.0 * curve * bend) * square))


def level_rows(level):
    high = level.astype(bf16).astype(f32)
    mid = (level - high).astype(bf16).astype(f32)
    low = (level - high - mid).astype(bf16).astype(f32)
    row = lax.broadcasted_iota(jnp.int32, (extra, level.shape[1]), 0)
    return jnp.where(row == 0, high, jnp.where(row == 1, mid, jnp.where(row == 2, low, 0.0)))


def widen(latent, level):
    return jnp.concatenate([latent.astype(f32), level_rows(level)], axis=0)


def norm_scale(wide, gram, width):
    seen = lax.dot_general(
        gram,
        wide,
        (((1,), (0,)), ((), ())),
        precision=lax.Precision.HIGHEST,
        preferred_element_type=f32,
    )
    square = jnp.maximum(jnp.sum(seen * wide, axis=0, keepdims=True), 0.0)
    return lax.rsqrt(square * (1.0 / width) + 1e-06), seen


def columns_of(at, tile):
    kept = lax.axis_index("fsdp") & 1
    base = tile * ((at % chains) + chains * (kept if at < chains else 1 - kept))
    return pl.ds(pl.multiple_of(base, tile), tile)


def part_kernel(embed_ref, vectors_ref, block_ref, *rest):
    *outs, embed, buffer, sems = rest
    place = lax.axis_index("fsdp")
    depth, cols = buffer.shape
    tile = cols // (2 * chains)
    own = slice(None)
    if embed_ref.shape[1] != depth:
        own = pl.ds(pl.multiple_of(place * depth, depth), depth)
    small = pltpu.make_async_copy(embed_ref.at[:, own], embed, sems.at[2 * chains])
    order = [*range(chains, 2 * chains), *range(chains)]
    large = [
        pltpu.make_async_copy(
            block_ref.at[0, :, columns_of(at, tile)],
            buffer.at[:, at * tile : (at + 1) * tile],
            sems.at[at],
        )
        for at in order
    ]
    small.start()
    for copy in large:
        copy.start()
    stamp, gain = vectors_ref[0:1, own], vectors_ref[1:2, own]
    row = lax.broadcasted_iota(jnp.int32, (extra, depth), 0)
    stamped = jnp.where(row < 3, stamp * gain, 0.0)
    small.wait()
    gained = jnp.concatenate([embed[...].astype(f32) * gain, stamped], axis=0)
    rows = gained.shape[0]
    both = jnp.concatenate([gained, gained - gained.astype(bf16).astype(f32)], axis=0).astype(bf16)
    outs[2 * chains][...] = both
    for at, copy in zip(order, large):
        copy.wait()
        part = mm(both, buffer[:, at * tile : (at + 1) * tile], 1, 0)
        outs[at][...] = (part[:rows] + part[rows:]).astype(outs[at].dtype)


def network(wide16, scale, proj_refs, first_piece, readout_ref, slope_ref=None):
    tile = proj_refs[0].shape[1]
    total = jnp.zeros((readout_ref.shape[0], wide16.shape[1]), f32)
    for at, proj_ref in enumerate(proj_refs, first_piece):
        hidden = scale * mm(proj_ref[...], wide16, 0, 0)
        gate, square = gelu_gate(hidden)
        activated = (hidden * gate).astype(bf16)
        total = total + mm(readout_ref[:, columns_of(at, tile)], activated, 1, 0)
        if slope_ref is not None:
            slope_ref[at * tile : (at + 1) * tile, :] = gelu_slope(hidden, square, gate)
    return total


def lanes_of_zeros(wide, lanes=128):
    return jnp.concatenate([wide, jnp.zeros((lanes - wide.shape[0], wide.shape[1]), f32)], axis=0)


def early_kernel(latent_ref, gram_ref, *rest, width):
    *proj_refs, readout_ref, total_ref = rest
    channels, tokens = latent_ref.shape

    @pl.when(lax.axis_index("role") == 0)
    def _():
        wide = widen(latent_ref[...], jnp.ones((1, tokens), f32))
        scale, unused = norm_scale(wide, gram_ref[...], width)
        total_ref[:channels, :] = network(wide.astype(bf16), scale, proj_refs, 0, readout_ref)
        total_ref[channels:, :] = jnp.broadcast_to(scale, (extra, tokens))


def late_kernel(latent_ref, noise_ref, level_ref, gram_ref, total_ref, *rest):
    *proj_refs, readout_ref, out_ref, mix_ref, gram_out_ref = rest
    channels, tokens = latent_ref.shape
    level = level_ref[...]
    mix_ref[:channels, :] = level * noise_ref[...].astype(f32)
    mix_ref[channels:, :] = jnp.broadcast_to(level, (extra, tokens))
    gram_out_ref[...] = gram_ref[...]

    @pl.when(lax.axis_index("role") == 0)
    def _():
        wide16 = widen(latent_ref[...], jnp.ones((1, tokens), f32)).astype(bf16)
        scale = total_ref[channels : channels + 1, :]
        total = network(wide16, scale, proj_refs, chains, readout_ref)
        out_ref[...] = (total_ref[:channels, :] + total).astype(bf16)


def slope_kernel(latent_ref, scaled_in_ref, gram_ref, own_ref, *rest, width):
    *proj_refs, own_turned_ref, slope_ref, scaled_ref = rest
    own_turned_ref[...] = lanes_of_zeros(own_ref[...].astype(f32), 256).T.astype(bf16)
    rows, tile = proj_refs[0].shape
    wide = widen(latent_ref[...], jnp.ones((1, latent_ref.shape[1]), f32))
    scale, unused = norm_scale(wide, gram_ref[...], width)
    scaled = jnp.where(lax.axis_index("role") == 0, scale * wide, scaled_in_ref[...])
    high, low = halves(scaled)
    scaled_ref[...] = jnp.concatenate([scaled, scaled - high.astype(f32)], axis=0).astype(bf16)
    for at, proj_ref in enumerate(proj_refs):
        hidden = mm(proj_ref[...], high, 0, 0) + mm(proj_ref[...], low, 0, 0)
        gate, square = gelu_gate(hidden)
        slope_ref[at * tile : (at + 1) * tile, :] = gelu_slope(hidden, square, gate)


def second_kernel(own_ref, by1_ref, by3_ref, by2_ref, mix_ref, gram_ref, *rest, width):
    proj_refs = rest[: 2 * chains]
    readout_ref, columns_ref, generated_ref, piece_ref, flat_ref, scaled_ref, slope_ref = rest[2 * chains :]
    role = lax.axis_index("role")
    channels, tokens = own_ref.shape
    tile = proj_refs[0].shape[1]
    low = jnp.where(role == 0, own_ref[...].astype(f32), by1_ref[...].astype(f32))
    high = jnp.where(role == 2, by2_ref[...].astype(f32), by3_ref[...].astype(f32))
    generated = jnp.where(role < 2, low, high)
    generated_ref[...] = generated.astype(bf16)

    def score(slope_ref):
        level = mix_ref[channels : channels + 1, :]
        noised = (1.0 - level) * generated + mix_ref[:channels, :]
        wide = widen(noised.astype(bf16), level)
        scale, seen = norm_scale(wide, gram_ref[...], width)
        scaled_ref[...] = scale * wide
        scores = network(wide.astype(bf16), scale, proj_refs, 0, readout_ref, slope_ref).astype(bf16)
        return level, wide, scale, seen, scores

    @pl.when((role == 1) | (role == 2))
    def _():
        piece_ref[...] = score(None)[4]

    @pl.when(role == 3)
    def _():
        level, wide, scale, seen, scores = score(slope_ref)
        logit = jnp.sum(scores.astype(f32), axis=0, keepdims=True)
        flat_ref[...] = 1.0 / (1.0 + jnp.exp(-logit))
        high, low = halves(-1.0 / (1.0 + jnp.exp(logit)))
        cot = jnp.concatenate(
            [
                jnp.broadcast_to(high, (channels, tokens)),
                jnp.broadcast_to(low, (channels, tokens)),
            ],
            axis=0,
        )
        back_rows = jnp.zeros(wide.shape, f32)
        for at, proj_ref in enumerate(proj_refs):
            back = mm(columns_ref[columns_of(at, tile), :], cot, 1, 0)
            hcot = (back * slope_ref[at * tile : (at + 1) * tile, :]).astype(bf16)
            back_rows = back_rows + mm(proj_ref[...], hcot, 1, 0)
        inner = scale * jnp.sum(back_rows * wide, axis=0, keepdims=True)
        latent_back = scale * back_rows[:channels] - (scale * scale * inner * (1.0 / width)) * seen[:channels]
        piece_ref[...] = (adv_weight * (1.0 - level) * latent_back).astype(bf16)


def pull_back(cot, tail, out_refs, first_piece):
    slope_ref, scaled_ref, columns_ref = tail
    rows, tile = out_refs[0].shape
    scaled = scaled_ref[...]
    for at, out_ref in enumerate(out_refs, first_piece):
        back = mm(columns_ref[columns_of(at, tile), :], cot, 1, 0)
        hcot = (back * slope_ref[at * tile : (at + 1) * tile, :]).astype(bf16)
        part = mm(scaled, hcot, 1, 1)
        out_ref[...] = (part[:rows] + part[rows:]).astype(out_ref.dtype)


def send_kernel(
    real_ref,
    adversarial_ref,
    fake_ref,
    generated_ref,
    piece_ref,
    flat_ref,
    *rest,
):
    tail, cot_ref, out_refs = rest[:3], rest[3], rest[4:]
    role = lax.axis_index("role")
    first = role == 0
    generated = generated_ref[...].astype(f32)
    piece = piece_ref[...].astype(f32)
    fake = fake_ref[...].astype(f32)
    real = real_ref[...].astype(f32)
    adversarial = adversarial_ref[...].astype(f32)
    spread = jnp.mean(jnp.abs(generated - real), axis=0, keepdims=True) + 1e-05
    dmd = (fake - real) / spread
    flat = jnp.broadcast_to(flat_ref[...], generated.shape)
    flat_high = flat.astype(bf16).astype(f32)
    left = jnp.where(
        first, dmd, jnp.where(role == 2, piece, jnp.where(role == 3, flat_high, 0.0))
    ).astype(bf16)
    right = jnp.where(
        first,
        adversarial,
        jnp.where(role == 2, -generated, jnp.where(role == 3, flat - flat_high, 0.0)),
    ).astype(bf16)
    cot = jnp.concatenate([left, right], axis=0)
    cot_ref[...] = cot
    pull_back(cot, tail, out_refs, chains)


def keep_kernel(cot_ref, *rest):
    pull_back(cot_ref[...], rest[:3], rest[3:], 0)


def grad_kernel(own_ref, *rest, factor, first_piece, count):
    total_refs = rest[:count]
    *unused, out_ref, buffer, sems = rest[count:]
    tile = buffer.shape[1] // count
    own = own_ref[...]
    copies = []
    for at, total_ref in enumerate(total_refs):
        here = slice(at * tile, (at + 1) * tile)
        total = total_ref[...].astype(f32)
        part = mm(own, lanes_of_zeros(jnp.concatenate([total, total], axis=0), 256).astype(bf16), 1, 0)
        buffer[:, here] = part * factor
        cols = columns_of(first_piece + at, tile)
        copy = pltpu.make_async_copy(buffer.at[:, here], out_ref.at[0, :, cols], sems.at[at])
        copy.start()
        copies.append(copy)
    for copy in copies:
        copy.wait()


def call(kernel, name, out_shape, inputs, scratch=(), cost=0):
    many = isinstance(out_shape, list)
    vmem = pl.BlockSpec(memory_space=pltpu.VMEM)
    return pl.pallas_call(
        kernel,
        out_shape=out_shape,
        in_specs=[vmem] * len(inputs),
        out_specs=[vmem] * len(out_shape) if many else vmem,
        scratch_shapes=list(scratch),
        compiler_params=pltpu.CompilerParams(vmem_limit_bytes=16 * 1024 * 1024),
        cost_estimate=pl.CostEstimate(flops=cost, bytes_accessed=cost // 1000, transcendentals=cost // 1000),
        name=name,
    )(*inputs)


def part_of(embed_w, vectors, block_weight):
    depth, cols = block_weight.shape[1:]
    channels = embed_w.shape[0]
    rows, tile = channels + extra, cols // (2 * chains)
    if depth % 128 != 0:
        embed_w, vectors = (
            lax.dynamic_slice_in_dim(value, lax.axis_index("fsdp") * depth, depth, 1)
            for value in (embed_w, vectors)
        )
    shapes = [jax.ShapeDtypeStruct((rows, tile), dtype) for dtype in (f32, bf16) for at in range(chains)]
    shapes.append(jax.ShapeDtypeStruct((2 * rows, depth), bf16))
    vmem = pl.BlockSpec(memory_space=pltpu.VMEM)
    hbm = pl.BlockSpec(memory_space=pltpu.HBM)
    return pl.pallas_call(
        part_kernel,
        out_shape=shapes,
        in_specs=[hbm, vmem, hbm],
        out_specs=[vmem] * len(shapes),
        scratch_shapes=[
            pltpu.VMEM((channels, depth), bf16),
            pltpu.VMEM((depth, cols), bf16),
            pltpu.SemaphoreType.DMA((2 * chains + 1,)),
        ],
        compiler_params=pltpu.CompilerParams(vmem_limit_bytes=part_limit * 1024),
        cost_estimate=pl.CostEstimate(
            flops=4 * rows * depth * cols, bytes_accessed=2 * depth * cols, transcendentals=0
        ),
        name="part",
    )(embed_w, vectors, block_weight)


def gradient(own, totals, first_piece, factor, cols, buffer=None):
    depth, tile, count = own.shape[0], cols // (2 * chains), len(totals)
    vmem = pl.BlockSpec(memory_space=pltpu.VMEM)
    hbm = pl.BlockSpec(memory_space=pltpu.HBM)
    specs = [vmem] * (1 + count)
    inputs = [own, *totals]
    if buffer is not None:
        specs.append(hbm)
        inputs.append(buffer)
    return pl.pallas_call(
        functools.partial(grad_kernel, factor=factor, first_piece=first_piece, count=count),
        out_shape=jax.ShapeDtypeStruct((1, depth, cols), f32),
        in_specs=specs,
        out_specs=hbm,
        input_output_aliases={} if buffer is None else {len(inputs) - 1: 0},
        scratch_shapes=[pltpu.VMEM((depth, count * tile), f32), pltpu.SemaphoreType.DMA((count,))],
        compiler_params=pltpu.CompilerParams(vmem_limit_bytes=16 * 1024 * 1024),
        cost_estimate=pl.CostEstimate(
            flops=2 * own.shape[1] * depth * count * tile,
            bytes_accessed=4 * depth * count * tile,
            transcendentals=0,
        ),
        name="gradient",
    )(*inputs)


def swap(value, axis, n, bit):
    return lax.ppermute(value, axis, [(i, i ^ bit) for i in range(n)])


def add_all(kept, sent, n):
    bits = [1 << at for at in range(n.bit_length() - 1)]
    mine = []
    for value, part in zip(kept, sent):
        for bit in bits:
            outgoing = part if bit == 1 else value.astype(bf16)
            value = value + swap(outgoing, "fsdp", n, bit).astype(f32)
        mine.append(value.astype(bf16))
    return mine, [swap(value, "fsdp", n, 1) for value in mine]


def shards(
    source_noise,
    score_noise,
    noise_level,
    embed_weight,
    time_vector,
    norm_gain,
    block_weight,
    readout_weight,
):
    role = lax.axis_index("role")
    n = lax.axis_size("fsdp")
    embed_w = embed_weight[0]
    readout = readout_weight[0].T
    depth, cols = block_weight.shape[1:]
    channels, width = embed_w.shape
    tokens = source_noise.shape[0]
    rows = channels + extra
    tile = cols // (2 * chains)
    shape = jax.ShapeDtypeStruct
    roles = lax.axis_size("role")

    vectors = jnp.concatenate([time_vector, norm_gain], axis=0)
    *parts, own_rows = part_of(embed_w, vectors, block_weight)
    mine, others = add_all(parts[:chains], parts[chains:], n)
    proj = mine + others

    tall = jnp.concatenate(
        [embed_w.astype(f32), jnp.broadcast_to(time_vector, (3, width)), jnp.zeros((extra - 3, width), f32)]
    )
    gram = jnp.dot(tall, tall.T, precision=lax.Precision.HIGHEST)
    columns = jnp.concatenate([readout, readout], axis=0).T
    level = noise_level[None, :]
    source = source_noise.T
    latent_shape = shape((channels, tokens), bf16)

    cost = 2 * rows * tokens * cols
    total = call(
        functools.partial(early_kernel, width=width),
        "generator_early",
        shape((rows, tokens), f32),
        (source, gram, *mine, readout),
        cost=cost,
    )
    own_first, mix, gram = call(
        late_kernel,
        "generator_late",
        [latent_shape, shape((rows, tokens), f32), shape((rows, rows), f32)],
        (source, score_noise.T, level, gram, total, *others, readout),
    )
    by2, by3, by1 = (swap(own_first, "role", roles, bit) for bit in (2, 3, 1))
    drawn = jnp.where(role == 0, own_first, jnp.where(role == 1, by1, jnp.where(role == 2, by2, by3)))
    generated, piece, flat, scaled = call(
        functools.partial(second_kernel, width=width),
        "score",
        [latent_shape, latent_shape, shape((1, tokens), f32), shape((rows, tokens), f32)],
        (own_first, by1, by3, by2, mix, gram, *proj, readout, columns),
        scratch=[pltpu.VMEM((cols, tokens), f32)],
    )
    fake, adversarial, real = (swap(piece, "role", roles, bit) for bit in (2, 3, 1))
    own_turned, slope, scaled = call(
        functools.partial(slope_kernel, width=width),
        "slopes",
        [shape((depth, 256), bf16), shape((cols, tokens), f32), shape((2 * rows, tokens), bf16)],
        (source, scaled, gram, own_rows, *proj),
        cost=cost,
    )
    flat, drawn = lax.optimization_barrier((flat, drawn))

    tail = (slope, scaled, columns)
    cot, *send = call(
        send_kernel,
        "cotangent_send",
        [shape((2 * channels, tokens), bf16)] + [shape((rows, tile), bf16)] * chains,
        (real, adversarial, fake, generated, piece, flat, *tail),
        cost=cost,
    )
    kept = call(
        keep_kernel, "cotangent_keep", [shape((rows, tile), f32)] * chains, (cot, *tail), cost=cost
    )
    totals, others = add_all(kept, send, n)
    factor = 1.0 / math.sqrt(tokens * n)
    grads = gradient(own_turned, totals, 0, factor, cols)
    for at, other in enumerate(others, chains):
        grads = gradient(own_turned, [other], at, factor, cols, grads)
    return (grads, drawn.T)


def solution(mesh):
    in_specs = (
        P("fsdp", None),
        P("fsdp", None),
        P("fsdp"),
        P("role", None, None),
        P("role", None),
        P("role", None),
        P("role", "fsdp", None),
        P("role", None, None),
    )
    out_specs = (P("role", "fsdp", None), P("fsdp", None))
    return jax.shard_map(shards, mesh=mesh, in_specs=in_specs, out_specs=out_specs, check_vma=False)
```

```python
import functools
import math

import jax
import jax.numpy as jnp
from jax import lax
from jax.experimental import pallas as pl
from jax.experimental.pallas import tpu as pltpu
from jax.sharding import PartitionSpec as P

adv_weight = 3.0
f32 = jnp.float32
bf16 = jnp.bfloat16
extra = 8
chains = 2
part_limit = 54528
curve = math.sqrt(2.0 / math.pi)
bend = 0.044715


def halves(value):
    high = value.astype(bf16)
    return high, (value - high.astype(f32)).astype(bf16)


def mm(left, right, left_dim, right_dim):
    return lax.dot_general(
        left, right, (((left_dim,), (right_dim,)), ((), ())), preferred_element_type=f32
    )


def gelu_gate(hidden):
    square = hidden * hidden
    return 0.5 + 0.5 * jnp.tanh(hidden * (curve + (curve * bend) * square)), square


def gelu_slope(hidden, square, gate):
    return gate + (gate - gate * gate) * (hidden * (2.0 * curve + (6.0 * curve * bend) * square))


def level_rows(level):
    high = level.astype(bf16).astype(f32)
    mid = (level - high).astype(bf16).astype(f32)
    low = (level - high - mid).astype(bf16).astype(f32)
    row = lax.broadcasted_iota(jnp.int32, (extra, level.shape[1]), 0)
    return jnp.where(row == 0, high, jnp.where(row == 1, mid, jnp.where(row == 2, low, 0.0)))


def widen(latent, level):
    return jnp.concatenate([latent.astype(f32), level_rows(level)], axis=0)


def norm_scale(wide, gram, width):
    seen = lax.dot_general(
        gram,
        wide,
        (((1,), (0,)), ((), ())),
        precision=lax.Precision.HIGHEST,
        preferred_element_type=f32,
    )
    square = jnp.maximum(jnp.sum(seen * wide, axis=0, keepdims=True), 0.0)
    return lax.rsqrt(square * (1.0 / width) + 1e-06), seen


def columns_of(at, tile):
    kept = lax.axis_index("fsdp") & 1
    base = tile * ((at % chains) + chains * (kept if at < chains else 1 - kept))
    return pl.ds(pl.multiple_of(base, tile), tile)


def part_kernel(embed_ref, vectors_ref, block_ref, *rest):
    *outs, embed, buffer, sems = rest
    place = lax.axis_index("fsdp")
    depth, cols = buffer.shape
    tile = cols // (2 * chains)
    own = slice(None)
    if embed_ref.shape[1] != depth:
        own = pl.ds(pl.multiple_of(place * depth, depth), depth)
    small = pltpu.make_async_copy(embed_ref.at[:, own], embed, sems.at[2 * chains])
    order = [*range(chains, 2 * chains), *range(chains)]
    large = [
        pltpu.make_async_copy(
            block_ref.at[0, :, columns_of(at, tile)],
            buffer.at[:, at * tile : (at + 1) * tile],
            sems.at[at],
        )
        for at in order
    ]
    small.start()
    for copy in large:
        copy.start()
    stamp, gain = vectors_ref[0:1, own], vectors_ref[1:2, own]
    row = lax.broadcasted_iota(jnp.int32, (extra, depth), 0)
    stamped = jnp.where(row < 3, stamp * gain, 0.0)
    small.wait()
    gained = jnp.concatenate([embed[...].astype(f32) * gain, stamped], axis=0)
    rows = gained.shape[0]
    both = jnp.concatenate([gained, gained - gained.astype(bf16).astype(f32)], axis=0).astype(bf16)
    outs[2 * chains][...] = both
    for at, copy in zip(order, large):
        copy.wait()
        part = mm(both, buffer[:, at * tile : (at + 1) * tile], 1, 0)
        outs[at][...] = (part[:rows] + part[rows:]).astype(outs[at].dtype)


def network(wide16, scale, proj_refs, first_piece, readout_ref, slope_ref=None):
    tile = proj_refs[0].shape[1]
    total = jnp.zeros((readout_ref.shape[0], wide16.shape[1]), f32)
    for at, proj_ref in enumerate(proj_refs, first_piece):
        hidden = scale * mm(proj_ref[...], wide16, 0, 0)
        gate, square = gelu_gate(hidden)
        activated = (hidden * gate).astype(bf16)
        total = total + mm(readout_ref[:, columns_of(at, tile)], activated, 1, 0)
        if slope_ref is not None:
            slope_ref[at * tile : (at + 1) * tile, :] = gelu_slope(hidden, square, gate)
    return total


def lanes_of_zeros(wide, lanes=128):
    return jnp.concatenate([wide, jnp.zeros((lanes - wide.shape[0], wide.shape[1]), f32)], axis=0)


def early_kernel(latent_ref, gram_ref, *rest, width):
    *proj_refs, readout_ref, total_ref = rest
    channels, tokens = latent_ref.shape

    @pl.when(lax.axis_index("role") == 0)
    def _():
        wide = widen(latent_ref[...], jnp.ones((1, tokens), f32))
        scale, unused = norm_scale(wide, gram_ref[...], width)
        total_ref[:channels, :] = network(wide.astype(bf16), scale, proj_refs, 0, readout_ref)
        total_ref[channels:, :] = jnp.broadcast_to(scale, (extra, tokens))


def late_kernel(latent_ref, noise_ref, level_ref, gram_ref, total_ref, *rest):
    *proj_refs, readout_ref, out_ref, mix_ref, gram_out_ref = rest
    channels, tokens = latent_ref.shape
    level = level_ref[...]
    mix_ref[:channels, :] = level * noise_ref[...].astype(f32)
    mix_ref[channels:, :] = jnp.broadcast_to(level, (extra, tokens))
    gram_out_ref[...] = gram_ref[...]

    @pl.when(lax.axis_index("role") == 0)
    def _():
        wide16 = widen(latent_ref[...], jnp.ones((1, tokens), f32)).astype(bf16)
        scale = total_ref[channels : channels + 1, :]
        total = network(wide16, scale, proj_refs, chains, readout_ref)
        out_ref[...] = (total_ref[:channels, :] + total).astype(bf16)


def slope_kernel(latent_ref, scaled_in_ref, gram_ref, own_ref, *rest, width):
    *proj_refs, own_turned_ref, slope_ref, scaled_ref = rest
    own_turned_ref[...] = lanes_of_zeros(own_ref[...].astype(f32), 256).T.astype(bf16)
    rows, tile = proj_refs[0].shape
    wide = widen(latent_ref[...], jnp.ones((1, latent_ref.shape[1]), f32))
    scale, unused = norm_scale(wide, gram_ref[...], width)
    scaled = jnp.where(lax.axis_index("role") == 0, scale * wide, scaled_in_ref[...])
    high, low = halves(scaled)
    scaled_ref[...] = jnp.concatenate([scaled, scaled - high.astype(f32)], axis=0).astype(bf16)
    for at, proj_ref in enumerate(proj_refs):
        hidden = mm(proj_ref[...], high, 0, 0) + mm(proj_ref[...], low, 0, 0)
        gate, square = gelu_gate(hidden)
        slope_ref[at * tile : (at + 1) * tile, :] = gelu_slope(hidden, square, gate)


def second_kernel(own_ref, by1_ref, by3_ref, by2_ref, mix_ref, gram_ref, *rest, width):
    proj_refs = rest[: 2 * chains]
    readout_ref, columns_ref, generated_ref, piece_ref, flat_ref, scaled_ref, slope_ref = rest[2 * chains :]
    role = lax.axis_index("role")
    channels, tokens = own_ref.shape
    tile = proj_refs[0].shape[1]
    low = jnp.where(role == 0, own_ref[...].astype(f32), by1_ref[...].astype(f32))
    high = jnp.where(role == 2, by2_ref[...].astype(f32), by3_ref[...].astype(f32))
    generated = jnp.where(role < 2, low, high)
    generated_ref[...] = generated.astype(bf16)

    def score(slope_ref):
        level = mix_ref[channels : channels + 1, :]
        noised = (1.0 - level) * generated + mix_ref[:channels, :]
        wide = widen(noised.astype(bf16), level)
        scale, seen = norm_scale(wide, gram_ref[...], width)
        scaled_ref[...] = scale * wide
        scores = network(wide.astype(bf16), scale, proj_refs, 0, readout_ref, slope_ref).astype(bf16)
        return level, wide, scale, seen, scores

    @pl.when((role == 1) | (role == 2))
    def _():
        piece_ref[...] = score(None)[4]

    @pl.when(role == 3)
    def _():
        level, wide, scale, seen, scores = score(slope_ref)
        logit = jnp.sum(scores.astype(f32), axis=0, keepdims=True)
        flat_ref[...] = 1.0 / (1.0 + jnp.exp(-logit))
        high, low = halves(-1.0 / (1.0 + jnp.exp(logit)))
        cot = jnp.concatenate(
            [
                jnp.broadcast_to(high, (channels, tokens)),
                jnp.broadcast_to(low, (channels, tokens)),
            ],
            axis=0,
        )
        back_rows = jnp.zeros(wide.shape, f32)
        for at, proj_ref in enumerate(proj_refs):
            back = mm(columns_ref[columns_of(at, tile), :], cot, 1, 0)
            hcot = (back * slope_ref[at * tile : (at + 1) * tile, :]).astype(bf16)
            back_rows = back_rows + mm(proj_ref[...], hcot, 1, 0)
        inner = scale * jnp.sum(back_rows * wide, axis=0, keepdims=True)
        latent_back = scale * back_rows[:channels] - (scale * scale * inner * (1.0 / width)) * seen[:channels]
        piece_ref[...] = (adv_weight * (1.0 - level) * latent_back).astype(bf16)


def pull_back(cot, tail, out_refs, first_piece):
    slope_ref, scaled_ref, columns_ref = tail
    rows, tile = out_refs[0].shape
    scaled = scaled_ref[...]
    for at, out_ref in enumerate(out_refs, first_piece):
        back = mm(columns_ref[columns_of(at, tile), :], cot, 1, 0)
        hcot = (back * slope_ref[at * tile : (at + 1) * tile, :]).astype(bf16)
        part = mm(scaled, hcot, 1, 1)
        out_ref[...] = (part[:rows] + part[rows:]).astype(out_ref.dtype)


def send_kernel(
    real_ref,
    adversarial_ref,
    fake_ref,
    generated_ref,
    piece_ref,
    flat_ref,
    *rest,
):
    tail, cot_ref, out_refs = rest[:3], rest[3], rest[4:]
    role = lax.axis_index("role")
    first = role == 0
    generated = generated_ref[...].astype(f32)
    piece = piece_ref[...].astype(f32)
    fake = fake_ref[...].astype(f32)
    real = real_ref[...].astype(f32)
    adversarial = adversarial_ref[...].astype(f32)
    spread = jnp.mean(jnp.abs(generated - real), axis=0, keepdims=True) + 1e-05
    dmd = (fake - real) / spread
    flat = jnp.broadcast_to(flat_ref[...], generated.shape)
    flat_high = flat.astype(bf16).astype(f32)
    left = jnp.where(
        first, dmd, jnp.where(role == 2, piece, jnp.where(role == 3, flat_high, 0.0))
    ).astype(bf16)
    right = jnp.where(
        first,
        adversarial,
        jnp.where(role == 2, -generated, jnp.where(role == 3, flat - flat_high, 0.0)),
    ).astype(bf16)
    cot = jnp.concatenate([left, right], axis=0)
    cot_ref[...] = cot
    pull_back(cot, tail, out_refs, chains)


def keep_kernel(cot_ref, *rest):
    pull_back(cot_ref[...], rest[:3], rest[3:], 0)


def grad_kernel(own_ref, *rest, factor, first_piece, count):
    total_refs = rest[:count]
    *unused, out_ref, buffer, sems = rest[count:]
    tile = buffer.shape[1] // count
    own = own_ref[...]
    copies = []
    for at, total_ref in enumerate(total_refs):
        here = slice(at * tile, (at + 1) * tile)
        total = total_ref[...].astype(f32)
        part = mm(own, lanes_of_zeros(jnp.concatenate([total, total], axis=0), 256).astype(bf16), 1, 0)
        buffer[:, here] = part * factor
        cols = columns_of(first_piece + at, tile)
        copy = pltpu.make_async_copy(buffer.at[:, here], out_ref.at[0, :, cols], sems.at[at])
        copy.start()
        copies.append(copy)
    for copy in copies:
        copy.wait()


def call(kernel, name, out_shape, inputs, scratch=(), cost=0):
    many = isinstance(out_shape, list)
    vmem = pl.BlockSpec(memory_space=pltpu.VMEM)
    return pl.pallas_call(
        kernel,
        out_shape=out_shape,
        in_specs=[vmem] * len(inputs),
        out_specs=[vmem] * len(out_shape) if many else vmem,
        scratch_shapes=list(scratch),
        compiler_params=pltpu.CompilerParams(vmem_limit_bytes=16 * 1024 * 1024),
        cost_estimate=pl.CostEstimate(flops=cost, bytes_accessed=cost // 1000, transcendentals=cost // 1000),
        name=name,
    )(*inputs)


def part_of(embed_w, vectors, block_weight):
    depth, cols = block_weight.shape[1:]
    channels = embed_w.shape[0]
    rows, tile = channels + extra, cols // (2 * chains)
    if depth % 128 != 0:
        embed_w, vectors = (
            lax.dynamic_slice_in_dim(value, lax.axis_index("fsdp") * depth, depth, 1)
            for value in (embed_w, vectors)
        )
    shapes = [jax.ShapeDtypeStruct((rows, tile), dtype) for dtype in (f32, bf16) for at in range(chains)]
    shapes.append(jax.ShapeDtypeStruct((2 * rows, depth), bf16))
    vmem = pl.BlockSpec(memory_space=pltpu.VMEM)
    hbm = pl.BlockSpec(memory_space=pltpu.HBM)
    return pl.pallas_call(
        part_kernel,
        out_shape=shapes,
        in_specs=[hbm, vmem, hbm],
        out_specs=[vmem] * len(shapes),
        scratch_shapes=[
            pltpu.VMEM((channels, depth), bf16),
            pltpu.VMEM((depth, cols), bf16),
            pltpu.SemaphoreType.DMA((2 * chains + 1,)),
        ],
        compiler_params=pltpu.CompilerParams(vmem_limit_bytes=part_limit * 1024),
        cost_estimate=pl.CostEstimate(
            flops=4 * rows * depth * cols, bytes_accessed=2 * depth * cols, transcendentals=0
        ),
        name="part",
    )(embed_w, vectors, block_weight)


def gradient(own, totals, first_piece, factor, cols, buffer=None):
    depth, tile, count = own.shape[0], cols // (2 * chains), len(totals)
    vmem = pl.BlockSpec(memory_space=pltpu.VMEM)
    hbm = pl.BlockSpec(memory_space=pltpu.HBM)
    specs = [vmem] * (1 + count)
    inputs = [own, *totals]
    if buffer is not None:
        specs.append(hbm)
        inputs.append(buffer)
    return pl.pallas_call(
        functools.partial(grad_kernel, factor=factor, first_piece=first_piece, count=count),
        out_shape=jax.ShapeDtypeStruct((1, depth, cols), f32),
        in_specs=specs,
        out_specs=hbm,
        input_output_aliases={} if buffer is None else {len(inputs) - 1: 0},
        scratch_shapes=[pltpu.VMEM((depth, count * tile), f32), pltpu.SemaphoreType.DMA((count,))],
        compiler_params=pltpu.CompilerParams(vmem_limit_bytes=16 * 1024 * 1024),
        cost_estimate=pl.CostEstimate(
            flops=2 * own.shape[1] * depth * count * tile,
            bytes_accessed=4 * depth * count * tile,
            transcendentals=0,
        ),
        name="gradient",
    )(*inputs)


def swap(value, axis, n, bit):
    return lax.ppermute(value, axis, [(i, i ^ bit) for i in range(n)])


def add_all(kept, sent, n):
    bits = [1 << at for at in range(n.bit_length() - 1)]
    mine = []
    for value, part in zip(kept, sent):
        for bit in bits:
            outgoing = part if bit == 1 else value.astype(bf16)
            value = value + swap(outgoing, "fsdp", n, bit).astype(f32)
        mine.append(value.astype(bf16))
    return mine, [swap(value, "fsdp", n, 1) for value in mine]


def shards(
    source_noise,
    score_noise,
    noise_level,
    embed_weight,
    time_vector,
    norm_gain,
    block_weight,
    readout_weight,
):
    role = lax.axis_index("role")
    n = lax.axis_size("fsdp")
    embed_w = embed_weight[0]
    readout = readout_weight[0].T
    depth, cols = block_weight.shape[1:]
    channels, width = embed_w.shape
    tokens = source_noise.shape[0]
    rows = channels + extra
    tile = cols // (2 * chains)
    shape = jax.ShapeDtypeStruct
    roles = lax.axis_size("role")

    vectors = jnp.concatenate([time_vector, norm_gain], axis=0)
    *parts, own_rows = part_of(embed_w, vectors, block_weight)
    mine, others = add_all(parts[:chains], parts[chains:], n)
    proj = mine + others

    tall = jnp.concatenate(
        [embed_w.astype(f32), jnp.broadcast_to(time_vector, (3, width)), jnp.zeros((extra - 3, width), f32)]
    )
    gram = jnp.dot(tall, tall.T, precision=lax.Precision.HIGHEST)
    columns = jnp.concatenate([readout, readout], axis=0).T
    level = noise_level[None, :]
    source = source_noise.T
    latent_shape = shape((channels, tokens), bf16)

    cost = 2 * rows * tokens * cols
    total = call(
        functools.partial(early_kernel, width=width),
        "generator_early",
        shape((rows, tokens), f32),
        (source, gram, *mine, readout),
        cost=cost,
    )
    own_first, mix, gram = call(
        late_kernel,
        "generator_late",
        [latent_shape, shape((rows, tokens), f32), shape((rows, rows), f32)],
        (source, score_noise.T, level, gram, total, *others, readout),
    )
    by2, by3, by1 = (swap(own_first, "role", roles, bit) for bit in (2, 3, 1))
    drawn = jnp.where(role == 0, own_first, jnp.where(role == 1, by1, jnp.where(role == 2, by2, by3)))
    generated, piece, flat, scaled = call(
        functools.partial(second_kernel, width=width),
        "score",
        [latent_shape, latent_shape, shape((1, tokens), f32), shape((rows, tokens), f32)],
        (own_first, by1, by3, by2, mix, gram, *proj, readout, columns),
        scratch=[pltpu.VMEM((cols, tokens), f32)],
    )
    fake = lax.ppermute(piece, "role", [(2, 0)])
    adversarial, real = (swap(piece, "role", roles, bit) for bit in (3, 1))
    own_turned, slope, scaled = call(
        functools.partial(slope_kernel, width=width),
        "slopes",
        [shape((depth, 256), bf16), shape((cols, tokens), f32), shape((2 * rows, tokens), bf16)],
        (source, scaled, gram, own_rows, *proj),
        cost=cost,
    )
    flat, drawn = lax.optimization_barrier((flat, drawn))

    tail = (slope, scaled, columns)
    cot, *send = call(
        send_kernel,
        "cotangent_send",
        [shape((2 * channels, tokens), bf16)] + [shape((rows, tile), bf16)] * chains,
        (real, adversarial, fake, generated, piece, flat, *tail),
        cost=cost,
    )
    kept = call(
        keep_kernel, "cotangent_keep", [shape((rows, tile), f32)] * chains, (cot, *tail), cost=cost
    )
    totals, others = add_all(kept, send, n)
    factor = 1.0 / math.sqrt(tokens * n)
    grads = gradient(own_turned, totals, 0, factor, cols)
    for at, other in enumerate(others, chains):
        grads = gradient(own_turned, [other], at, factor, cols, grads)
    return (grads, drawn.T)


def solution(mesh):
    in_specs = (
        P("fsdp", None),
        P("fsdp", None),
        P("fsdp"),
        P("role", None, None),
        P("role", None),
        P("role", None),
        P("role", "fsdp", None),
        P("role", None, None),
    )
    out_specs = (P("role", "fsdp", None), P("fsdp", None))
    return jax.shard_map(shards, mesh=mesh, in_specs=in_specs, out_specs=out_specs, check_vma=False)
```
